128 devices in a mesh: chan: 16 (over y_lo, z, core), freq: 8 (over x, y_hi).
Axes of the slice: x: 4, y: 4 (y_hi: 2, y_lo: 2; y = y_hi * 2 + y_lo), z: 4, core: 2. Of those that a mesh axis runs over, the one named last changes fastest.
Arguments:
- records: bfloat16 [18432, 5120], P(('chan', 'freq')), may hold values from -6 to 6
- offsets: int32 [8], replicated, may hold values from 0 to 14336, as said below
- sources: int32 [64], replicated, may hold values from 0 to 5119
Outputs:
- cross_spectra: bfloat16 [2, 64, 5120, 2048], P(None, None, 'chan', 'freq')
The draws below stay inside these ranges and needn't reach their ends.
Inputs may be any that keep to these rules, and one draw needn't show every extreme that they name: offsets never fall; the first is 0 and the last is 14336.
All inputs are finite; a program needn't handle non-finite values.
Results may differ from the reference program's by a relative error of at most 0.0068.
Values may be sent and summed in bfloat16 or wider, within the bound.
No kernel may reach another device: no remote copies, remote signals or barrier semaphores. Data moves between devices by JAX's collectives and lax.ppermute only.
A program may use at most 320 MiB of HBM per device.

```python
import jax
import jax.numpy as jnp
from jax import lax

NF = 2048
SEG = 8
NSRC = 64
HW = 32
CH = 5120
R = 18432


def draw_offsets(key, part):
    key = jax.random.fold_in(key, 5)
    inner = jax.random.randint(key, (SEG - 2,), 0, R - 2 * NF + 1, dtype=jnp.int32)
    inner = jnp.sort(inner)
    first = jnp.zeros((1,), jnp.int32)
    last = jnp.full((1,), R - 2 * NF, jnp.int32)
    return jnp.concatenate([first, inner, last])


def set_ends(result, rng, smallest, top_value):
    spot = [jax.random.randint(jax.random.fold_in(rng, axis), (), 0, length) for axis, length in enumerate(result.shape)]
    longest = result.shape.index(max(result.shape))
    beside = spot[:longest] + [(spot[longest] + 1) % result.shape[longest]] + spot[longest + 1:]
    return result.at[tuple(spot)].set(smallest).at[tuple(beside)].set(top_value)


def block_scale(rng, shape, shards, low, high):
    loudness = 1.0
    for position, shards_of in shards:
        steps = jax.random.uniform(jax.random.fold_in(jax.random.fold_in(rng, 6), position), (shards_of,), jnp.float32, low / len(shards), high / len(shards))
        loudness = loudness * jnp.repeat(jnp.exp(steps), shape[position] // shards_of).reshape((-1,) + (1,) * (len(shape) - 1 - position))
    return loudness


def gaussian(stream_key, dims, spread, reach, cuts=(), kind=jnp.bfloat16):
    array = spread * jax.random.normal(stream_key, dims, jnp.float32)
    if cuts:
        array = array * block_scale(stream_key, dims, cuts, -0.22, 0.18)
    return jnp.clip(array, -reach, reach).astype(kind)


def setup_inputs(seed: int = 0) -> dict:
    seeds = jax.random.split(jax.random.key(seed), 4)
    return {
        "records": gaussian(seeds[0], (R, CH), 1.0, 6.0, ((0, 128),)),
        "offsets": draw_offsets(jax.random.fold_in(seeds[3], 71), 0),
        "sources": set_ends(jax.random.randint(seeds[2], (NSRC,), 0, CH), jax.random.fold_in(seeds[2], 1), 0, CH - 1).astype(jnp.int32),
    }


EPSILON = 1e-06

def taper_window(length):
    steps = jnp.arange(length, dtype=jnp.int32).astype(jnp.float32)
    return 0.5 - 0.5 * jnp.cos(2.0 * jnp.pi * steps / length)

def fourier_table(freqs):
    length = 2 * freqs
    times = jnp.arange(length, dtype=jnp.int32)
    bins = jnp.arange(freqs, dtype=jnp.int32)
    angle = (times[:, None] * bins[None, :] % length).astype(jnp.float32) * (2.0 * jnp.pi / length)
    return jnp.concatenate([jnp.cos(angle), -jnp.sin(angle)], axis=1).astype(jnp.bfloat16)

def band_matrix(freqs, half):
    rows = jnp.arange(freqs, dtype=jnp.int32)
    inside = jnp.abs(rows[:, None] - rows[None, :]) <= half
    return (inside.astype(jnp.bfloat16), lax.optimization_barrier(jnp.sum(inside.astype(jnp.float32), axis=0)))

def whiten(spectrum, band, counts):
    real_part = spectrum[..., :NF]
    imag_part = spectrum[..., NF:]
    magnitude = jnp.sqrt(real_part * real_part + imag_part * imag_part).astype(jnp.bfloat16)
    smooth = jnp.dot(magnitude, band, preferred_element_type=jnp.float32)
    divisor = smooth / counts + EPSILON
    return jnp.stack([real_part / divisor, imag_part / divisor], axis=-2).astype(jnp.bfloat16)

def reference(records, offsets, sources):
    length = 2 * NF
    window = taper_window(length)
    table = fourier_table(NF)
    band, counts = band_matrix(NF, HW)

    def one_segment(start):
        piece = lax.dynamic_slice_in_dim(records, start.astype(jnp.int32), length, 0)
        tapered = (piece.astype(jnp.float32) * window[:, None]).astype(jnp.bfloat16)
        spectrum = jnp.dot(tapered.T, table, preferred_element_type=jnp.float32)
        return whiten(spectrum, band, counts)
    whitened = lax.map(one_segment, offsets)
    picked = whitened[:, sources]
    source_real = jnp.transpose(picked[:, :, 0].astype(jnp.float32), (1, 0, 2))
    source_imag = jnp.transpose(picked[:, :, 1].astype(jnp.float32), (1, 0, 2))
    white_real = whitened[:, :, 0].astype(jnp.float32)
    white_imag = whitened[:, :, 1].astype(jnp.float32)

    def one_source(pair):
        sreal, simag = pair
        real_sum = lax.optimization_barrier(jnp.sum(sreal[:, None, :] * white_real + simag[:, None, :] * white_imag, axis=0))
        imag_sum = lax.optimization_barrier(jnp.sum(sreal[:, None, :] * white_imag - simag[:, None, :] * white_real, axis=0))
        return (jnp.stack([real_sum, imag_sum]) * (1.0 / SEG)).astype(jnp.bfloat16)
    stacked = lax.map(one_source, (source_real, source_imag))
    return jnp.transpose(stacked, (1, 0, 2, 3))
```

```python
import numpy as np
import jax
import jax.numpy as jnp
import ml_dtypes
from jax import lax
from jax.experimental import pallas as pl
from jax.experimental.pallas import tpu as pltpu
from jax.sharding import PartitionSpec as P

NF = 2048
LENGTH = 2 * NF
SEG = 8
NSRC = 64
HW = 32
EPSILON = 1e-06

DEVICES = 128
ROWS = 144
OWN = 40
PICKED = 8
CHANS = OWN + PICKED
LANES = SEG * CHANS
BANDS = 8
WIDTH = 256
THIRD = ROWS // 3
VMEM = 56 * 1024 * 1024

NT = (((1,), (1,)), ((), ()))


def step_tables():
    a = np.arange(256)
    first = np.zeros((256, 256))
    for g in range(16):
        for i in range(8):
            f1 = 8 * g + i
            first[16 * g + i] = np.cos(2 * np.pi * ((a * f1) % 256) / 256)
            first[16 * g + 8 + i] = -np.sin(2 * np.pi * ((a * f1) % 256) / 256)
    first[8] = np.cos(np.pi * a)
    b = np.arange(16)
    second = np.zeros((16, 256, 256))
    for g in range(16):
        for band in range(BANDS):
            for j in range(16):
                if j < 8:
                    low = 8 * g + j
                elif g == 0:
                    low = 128 if j == 15 else 249 + j - 8
                else:
                    low = 249 - 8 * g + j - 8
                f = 256 * band + low
                angle = 2 * np.pi * ((b * f) % 4096) / 4096
                c, s = np.cos(angle), np.sin(angle)
                if low <= 128:
                    sign, slot = 1.0, low - 8 * g
                else:
                    sign, slot = -1.0, 256 - low - 8 * g
                row = (band * 2) * 16 + j
                if low == 0:
                    second[g, row, 16 * b] = c
                    second[g, row + 16, 16 * b] = -s
                elif low == 128:
                    second[g, row, 16 * b + 8] = c
                    second[g, row + 16, 16 * b + 8] = -s
                else:
                    second[g, row, 16 * b + slot] = c
                    second[g, row, 16 * b + 8 + slot] = sign * s
                    second[g, row + 16, 16 * b + slot] = -s
                    second[g, row + 16, 16 * b + 8 + slot] = sign * c
    return first.astype(ml_dtypes.bfloat16), second.astype(ml_dtypes.bfloat16)


def window_tables():
    a = np.arange(256) * (2 * np.pi / 256)
    b = np.arange(16) * (2 * np.pi / 4096)
    rows = np.stack([np.cos(a), np.sin(a)])[:, :, None] * np.ones((1, 1, 128))
    return rows.astype(np.float32), np.stack([np.cos(b), np.sin(b)]).astype(np.float32)


def band_block():
    rows = np.arange(128)[:, None] + 64
    return (np.abs(rows - np.arange(256)[None, :]) <= HW).astype(ml_dtypes.bfloat16)


def lane(shape):
    return lax.broadcasted_iota(jnp.int32, shape, 1)


def pack_kernel(sources_ref, records_ref, out_ref, head_ref, tail_ref):
    picked = jnp.zeros((ROWS, 128), jnp.float32)
    for i in range(8):
        cols = lane((128, 640)) + 640 * i
        hot = (cols == sources_ref[...]).astype(jnp.bfloat16)
        picked += lax.dot_general(records_ref[:, 640 * i:640 * i + 640], hot, NT, preferred_element_type=jnp.float32)
    at8 = lane((8, 128))
    for band in range(BANDS):
        head_ref[band] = pltpu.roll(picked[:THIRD], (120 - 8 * band) % 128, 1)
        tail = jnp.zeros((8, 128), jnp.float32)
        for m in range(12):
            piece = pltpu.roll(picked[THIRD + 8 * m:THIRD + 8 * m + 8], (8 * m - 8 * band) % 128, 1)
            tail = jnp.where((at8 >= 8 * m) & (at8 < 8 * m + 8), piece, tail)
        tail_ref[band] = tail
    at = lane((THIRD, 128))

    def group(i, carry):
        for j in range(16):
            tile, start = divmod(OWN * j, 128)
            parts = []
            for u in range(3):
                shift = (OWN * u - start) % 128

                def piece(t):
                    base = pl.multiple_of(640 * i + 128 * t, 128)
                    x = records_ref[THIRD * u:THIRD * u + THIRD, pl.ds(base, 128)].astype(jnp.float32)
                    return pltpu.roll(x, shift, 1) if shift else x
                part = piece(tile)
                if start + OWN > 128:
                    part = jnp.where(at >= OWN * u + 128 - start, piece(tile + 1), part)
                parts.append(part)
            main = jnp.where(at < 40, parts[0], jnp.where(at < 80, parts[1], jnp.where(at < 120, parts[2], head_ref[j % 8])))
            out_ref[16 * i + j] = jnp.concatenate([main, tail_ref[j % 8]], axis=0).astype(jnp.bfloat16)
        return carry
    lax.fori_loop(0, 8, group, 0)


def spectrum_kernel(offsets_ref, fine_ref, got_ref, first_ref, second_ref, band_ref, coarse_ref, out_ref,
                    time_ref, x_ref, y_ref, spec_ref, mag_ref):
    own48 = lane((THIRD, 128)) < OWN

    def unpack(src, carry):
        block = got_ref[src].astype(jnp.float32)
        main, tail = block[:THIRD], block[THIRD:]
        by48 = pltpu.roll(main, 48, 1)
        by88 = pltpu.roll(main, 88, 1)
        tails = [pltpu.roll(tail, (OWN - 8 * m) % 128, 1) for m in range(12)]
        base = pl.multiple_of(src * ROWS, 8)
        time_ref[pl.ds(base, THIRD)] = jnp.where(own48, main, by48)
        time_ref[pl.ds(base + THIRD, THIRD)] = jnp.where(own48, by88, jnp.concatenate(tails[:6], axis=0))
        time_ref[pl.ds(base + 2 * THIRD, THIRD)] = jnp.where(own48, by48, jnp.concatenate(tails[6:], axis=0))
        return carry
    lax.fori_loop(0, DEVICES, unpack, 0)

    at = lane((64, 128))

    def residue(b, carry):
        cb, sb = fine_ref[0, b], fine_ref[1, b]
        for chunk in range(4):
            rows = slice(64 * chunk, 64 * chunk + 64)
            window = 0.5 - 0.5 * (coarse_ref[0, rows] * cb - coarse_ref[1, rows] * sb)
            placed = []
            for k in range(SEG):
                start = offsets_ref[k] + b + 1024 * chunk
                piece = time_ref[pl.ds(start, 64, 16)] * window
                shift = (CHANS * k) % 128
                placed.append(pltpu.roll(piece, shift, 1) if shift else piece)
            t0 = jnp.where(at < 48, placed[0], jnp.where(at < 96, placed[1], placed[2]))
            t1 = jnp.where(at < 16, placed[2], jnp.where(at < 64, placed[3], jnp.where(at < 112, placed[4], placed[5])))
            t2 = jnp.where(at < 32, placed[5], jnp.where(at < 80, placed[6], placed[7]))
            x_ref[rows] = jnp.concatenate([t0, t1, t2], axis=1).astype(jnp.bfloat16)
        y = jnp.dot(first_ref[...], x_ref[...], preferred_element_type=jnp.float32).astype(jnp.bfloat16)
        base = pl.multiple_of(16 * b, 16)
        for g in range(16):
            y_ref[g, pl.ds(base, 16)] = y[16 * g:16 * g + 16]
        return carry
    lax.fori_loop(0, 16, residue, 0)

    for g in range(16):
        z = jnp.dot(second_ref[g], y_ref[g], preferred_element_type=jnp.float32)
        for band in range(BANDS):
            for p in range(2):
                r = (band * 2 + p) * 16
                base = 256 * band
                spec_ref[p, base + 8 * g:base + 8 * g + 8] = z[r:r + 8]
                if g == 0:
                    spec_ref[p, base + 249:base + 256] = z[r + 8:r + 15]
                    spec_ref[p, base + 128:base + 129] = z[r + 15:r + 16]
                else:
                    spec_ref[p, base + 249 - 8 * g:base + 257 - 8 * g] = z[r + 8:r + 16]

    mag_ref[0:64] = jnp.zeros((64, LANES), jnp.bfloat16)
    mag_ref[64 + NF:128 + NF] = jnp.zeros((64, LANES), jnp.bfloat16)

    def magnitude(i, carry):
        rows = pl.ds(pl.multiple_of(i * 64, 64), 64)
        re, im = spec_ref[0, rows], spec_ref[1, rows]
        mag_ref[pl.ds(pl.multiple_of(i * 64 + 64, 64), 64)] = jnp.sqrt(re * re + im * im).astype(jnp.bfloat16)
        return carry
    lax.fori_loop(0, NF // 64, magnitude, 0)

    def whiten(band, carry):
        for half in range(2):
            base = pl.multiple_of(band * 256 + 128 * half, 128)
            total = jnp.dot(band_ref[...], mag_ref[pl.ds(base, 256)], preferred_element_type=jnp.float32)
            f = base + lax.broadcasted_iota(jnp.int32, (128, LANES), 0)
            count = (jnp.minimum(f + HW, NF - 1) - jnp.maximum(f - HW, 0) + 1).astype(jnp.float32)
            scale = count / (total + EPSILON * count)
            for p in range(2):
                white = spec_ref[p, pl.ds(base, 128)] * scale
                for t in range(3):
                    turned = jnp.transpose(white[:, 128 * t:128 * t + 128])
                    out_ref[band, p, 128 * t:128 * t + 128, 128 * half:128 * half + 128] = turned.astype(jnp.bfloat16)
        return carry
    lax.fori_loop(0, BANDS, whiten, 0)


def diagonals(arrays, at):
    for bit in (1, 2, 4):
        odd = ((at // 16) & bit) != 0
        arrays = [jnp.where(odd, arrays[(i + bit) % 8], arrays[i]) for i in range(8)]
    return arrays


def cross_kernel(got_ref, out_ref, wide_ref, left_ref, picked_ref, weight_ref, prod_ref):
    step = pl.program_id(0)
    chans = BANDS * OWN

    @pl.when(step == 0)
    def _():
        at = lane((CHANS, 128))

        def gather(src, carry):
            for p in range(2):
                for h in range(2):
                    cols = slice(128 * h, 128 * h + 128)
                    arrays = []
                    for k in range(SEG):
                        x = got_ref[src, p, CHANS * k:CHANS * k + CHANS, cols].astype(jnp.float32)
                        arrays.append(pltpu.roll(x, 16 * k, 1) if k else x)
                    arrays = diagonals(arrays, at)
                    for g in range(8):
                        x = arrays[-g % 8]
                        wide_ref[8 * h + g, pl.ds(pl.multiple_of(OWN * src, 8), OWN), 128 * p:128 * p + 128] = x[:OWN]
                        picked_ref[8 * h + g, pl.ds(pl.multiple_of(PICKED * src, 8), PICKED), 128 * p:128 * p + 128] = x[OWN:] * (1.0 / SEG)
            return carry
        lax.fori_loop(0, BANDS, gather, 0)

        def narrow(g, carry):
            left_ref[g] = wide_ref[g].astype(jnp.bfloat16)
            return carry
        lax.fori_loop(0, 16, narrow, 0)

    same = (lane((16, 256)) % 16) == lax.broadcasted_iota(jnp.int32, (16, 256), 0)
    at = lane((16, 128))
    for h in range(2):
        for g in range(8):
            rows = picked_ref[8 * h + g, pl.ds(pl.multiple_of(8 * step, 8), 8)]
            turned = jnp.concatenate([-rows[:, 128:], rows[:, :128]], axis=1)
            for i in range(8):
                q = (i + g) % 8
                for p, values in ((0, rows), (1, turned)):
                    wide = jnp.where(same, jnp.broadcast_to(values[i:i + 1], (16, 256)), 0.0)
                    weight_ref[g, 128 * p + 16 * q:128 * p + 16 * q + 16] = wide.astype(jnp.bfloat16)
            prod_ref[g] = lax.dot_general(left_ref[8 * h + g], weight_ref[g], NT, preferred_element_type=jnp.float32)

        def place(c, carry):
            rows = pl.ds(pl.multiple_of(16 * c, 16), 16)
            for p in range(2):
                arrays = diagonals([prod_ref[g, rows, 128 * p:128 * p + 128] for g in range(8)], at)
                for i in range(8):
                    x = arrays[-i % 8]
                    x = pltpu.roll(x, (-16 * i) % 128, 1) if i else x
                    out_ref[p, i, rows, 128 * h:128 * h + 128] = x.astype(jnp.bfloat16)
            return carry
        lax.fori_loop(0, chans // 16, place, 0)


def whole(memory_space=pltpu.VMEM):
    return pl.BlockSpec(memory_space=memory_space)


def shards(records, offsets, sources):
    first, second = step_tables()
    coarse, fine = window_tables()
    columns = jnp.concatenate([sources, jnp.full((128 - NSRC,), -1, jnp.int32)])[:, None]
    blocks = pl.pallas_call(
        pack_kernel,
        out_shape=jax.ShapeDtypeStruct((DEVICES, 56, 128), jnp.bfloat16),
        in_specs=[whole(), whole()],
        out_specs=whole(),
        scratch_shapes=[pltpu.VMEM((8, THIRD, 128), jnp.float32), pltpu.VMEM((8, 8, 128), jnp.float32)],
        compiler_params=pltpu.CompilerParams(vmem_limit_bytes=VMEM),
        name="pack",
    )(columns, records)
    received = lax.all_to_all(blocks, ("chan", "freq"), split_axis=0, concat_axis=0, tiled=True)
    white = pl.pallas_call(
        spectrum_kernel,
        out_shape=jax.ShapeDtypeStruct((BANDS, 2, LANES, WIDTH), jnp.bfloat16),
        in_specs=[whole(pltpu.SMEM), whole(pltpu.SMEM)] + [whole()] * 5,
        out_specs=whole(),
        scratch_shapes=[
            pltpu.VMEM((ROWS * DEVICES, 128), jnp.float32),
            pltpu.VMEM((256, LANES), jnp.bfloat16),
            pltpu.VMEM((16, 256, LANES), jnp.bfloat16),
            pltpu.VMEM((2, NF, LANES), jnp.float32),
            pltpu.VMEM((NF + 128, LANES), jnp.bfloat16),
        ],
        compiler_params=pltpu.CompilerParams(vmem_limit_bytes=VMEM),
        name="spectrum",
    )(offsets, fine, received, first, second, band_block(), coarse)
    bands = lax.all_to_all(white, "freq", split_axis=0, concat_axis=0, tiled=True)
    chans = BANDS * OWN
    return pl.pallas_call(
        cross_kernel,
        out_shape=jax.ShapeDtypeStruct((2, NSRC, chans, WIDTH), jnp.bfloat16),
        grid=(NSRC // 8,),
        in_specs=[whole()],
        out_specs=pl.BlockSpec((2, 8, chans, WIDTH), lambda s: (0, s, 0, 0)),
        scratch_shapes=[
            pltpu.VMEM((16, chans, 256), jnp.float32),
            pltpu.VMEM((16, chans, 256), jnp.bfloat16),
            pltpu.VMEM((16, NSRC, 256), jnp.float32),
            pltpu.VMEM((8, 256, 256), jnp.bfloat16),
            pltpu.VMEM((8, chans, 256), jnp.float32),
        ],
        compiler_params=pltpu.CompilerParams(vmem_limit_bytes=VMEM),
        name="cross",
    )(bands)


def solution(mesh):
    in_specs = (P(("chan", "freq"), None), P(), P())
    out_specs = P(None, None, "chan", "freq")
    return jax.shard_map(shards, mesh=mesh, in_specs=in_specs, out_specs=out_specs, check_vma=False)
```

```python
import numpy as np
import jax
import jax.numpy as jnp
import ml_dtypes
from jax import lax
from jax.experimental import pallas as pl
from jax.experimental.pallas import tpu as pltpu
from jax.sharding import PartitionSpec as P

NF = 2048
LENGTH = 2 * NF
SEG = 8
NSRC = 64
HW = 32
EPSILON = 1e-06

DEVICES = 128
ROWS = 144
OWN = 40
PICKED = 8
CHANS = OWN + PICKED
LANES = SEG * CHANS
BANDS = 8
WIDTH = 256
THIRD = ROWS // 3
VMEM = 56 * 1024 * 1024

NT = (((1,), (1,)), ((), ()))


def step_tables():
    a = np.arange(256)
    first = np.zeros((256, 256))
    for g in range(16):
        for i in range(8):
            f1 = 8 * g + i
            first[16 * g + i] = np.cos(2 * np.pi * ((a * f1) % 256) / 256)
            first[16 * g + 8 + i] = -np.sin(2 * np.pi * ((a * f1) % 256) / 256)
    first[8] = np.cos(np.pi * a)
    b = np.arange(16)
    second = np.zeros((16, 256, 256))
    for g in range(16):
        for band in range(BANDS):
            for j in range(16):
                if j < 8:
                    low = 8 * g + j
                elif g == 0:
                    low = 128 if j == 15 else 249 + j - 8
                else:
                    low = 249 - 8 * g + j - 8
                f = 256 * band + low
                angle = 2 * np.pi * ((b * f) % 4096) / 4096
                c, s = np.cos(angle), np.sin(angle)
                if low <= 128:
                    sign, slot = 1.0, low - 8 * g
                else:
                    sign, slot = -1.0, 256 - low - 8 * g
                row = (band * 2) * 16 + j
                if low == 0:
                    second[g, row, 16 * b] = c
                    second[g, row + 16, 16 * b] = -s
                elif low == 128:
                    second[g, row, 16 * b + 8] = c
                    second[g, row + 16, 16 * b + 8] = -s
                else:
                    second[g, row, 16 * b + slot] = c
                    second[g, row, 16 * b + 8 + slot] = sign * s
                    second[g, row + 16, 16 * b + slot] = -s
                    second[g, row + 16, 16 * b + 8 + slot] = sign * c
    return first.astype(ml_dtypes.bfloat16), second.astype(ml_dtypes.bfloat16)


def window_tables():
    a = np.arange(256) * (2 * np.pi / 256)
    b = np.arange(16) * (2 * np.pi / 4096)
    rows = np.stack([np.cos(a), np.sin(a)])[:, :, None] * np.ones((1, 1, 128))
    return rows.astype(np.float32), np.stack([np.cos(b), np.sin(b)]).astype(np.float32)


def band_block():
    rows = np.arange(128)[:, None] + 64
    return (np.abs(rows - np.arange(256)[None, :]) <= HW).astype(ml_dtypes.bfloat16)


def lane(shape):
    return lax.broadcasted_iota(jnp.int32, shape, 1)


def pack_kernel(sources_ref, records_ref, out_ref, head_ref, tail_ref):
    picked = jnp.zeros((ROWS, NSRC), jnp.float32)
    for i in range(8):
        rows = lax.broadcasted_iota(jnp.int32, (640, NSRC), 0) + 640 * i
        hot = (rows == sources_ref[...]).astype(jnp.bfloat16)
        picked += jnp.dot(records_ref[:, 640 * i:640 * i + 640], hot, preferred_element_type=jnp.float32)
    picked = jnp.concatenate([picked, jnp.zeros((ROWS, 128 - NSRC), jnp.float32)], axis=1)
    at8 = lane((8, 128))
    for band in range(BANDS):
        head_ref[band] = pltpu.roll(picked[:THIRD], (120 - 8 * band) % 128, 1)
        tail = jnp.zeros((8, 128), jnp.float32)
        for m in range(12):
            piece = pltpu.roll(picked[THIRD + 8 * m:THIRD + 8 * m + 8], (8 * m - 8 * band) % 128, 1)
            tail = jnp.where((at8 >= 8 * m) & (at8 < 8 * m + 8), piece, tail)
        tail_ref[band] = tail
    at = lane((THIRD, 128))

    def group(i, carry):
        for j in range(16):
            tile, start = divmod(OWN * j, 128)
            parts = []
            for u in range(3):
                shift = (OWN * u - start) % 128

                def piece(t):
                    base = pl.multiple_of(640 * i + 128 * t, 128)
                    x = records_ref[THIRD * u:THIRD * u + THIRD, pl.ds(base, 128)].astype(jnp.float32)
                    return pltpu.roll(x, shift, 1) if shift else x
                part = piece(tile)
                if start + OWN > 128:
                    part = jnp.where(at >= OWN * u + 128 - start, piece(tile + 1), part)
                parts.append(part)
            main = jnp.where(at < 40, parts[0], jnp.where(at < 80, parts[1], jnp.where(at < 120, parts[2], head_ref[j % 8])))
            out_ref[16 * i + j] = jnp.concatenate([main, tail_ref[j % 8]], axis=0).astype(jnp.bfloat16)
        return carry
    lax.fori_loop(0, 8, group, 0)


def spectrum_kernel(offsets_ref, fine_ref, got_ref, first_ref, second_ref, band_ref, coarse_ref, out_ref,
                    time_ref, x_ref, y_ref, spec_ref, mag_ref):
    own48 = lane((THIRD, 128)) < OWN

    def unpack(src, carry):
        block = got_ref[src].astype(jnp.float32)
        main, tail = block[:THIRD], block[THIRD:]
        by48 = pltpu.roll(main, 48, 1)
        by88 = pltpu.roll(main, 88, 1)
        tails = [pltpu.roll(tail, (OWN - 8 * m) % 128, 1) for m in range(12)]
        thirds = [
            jnp.where(own48, main, by48),
            jnp.where(own48, by88, jnp.concatenate(tails[:6], axis=0)),
            jnp.where(own48, by48, jnp.concatenate(tails[6:], axis=0)),
        ]
        for i in range(9):
            time_ref[pl.ds(src * 153 + 17 * i, 16)] = thirds[i // 3][16 * (i % 3):16 * (i % 3) + 16]
        return carry
    lax.fori_loop(0, DEVICES, unpack, 0, unroll=8)

    at = lane((64, 128))

    def residues(quad, carry):
        for j in range(4):
            b = 4 * quad + j
            cb, sb = fine_ref[0, b], fine_ref[1, b]
            starts = [offsets_ref[k] + b for k in range(SEG)]
            starts = [start + lax.shift_right_logical(start, 4) for start in starts]
            for chunk in range(4):
                rows = slice(64 * chunk, 64 * chunk + 64)
                window = 0.5 - 0.5 * (coarse_ref[0, rows] * cb - coarse_ref[1, rows] * sb)
                placed = []
                for k in range(SEG):
                    piece = time_ref[pl.ds(starts[k] + 17 * 64 * chunk, 64, 17)] * window
                    shift = (CHANS * k) % 128
                    placed.append(pltpu.roll(piece, shift, 1) if shift else piece)
                t0 = jnp.where(at < 48, placed[0], jnp.where(at < 96, placed[1], placed[2]))
                t1 = jnp.where(at < 16, placed[2], jnp.where(at < 64, placed[3], jnp.where(at < 112, placed[4], placed[5])))
                t2 = jnp.where(at < 32, placed[5], jnp.where(at < 80, placed[6], placed[7]))
                x_ref[j, rows] = jnp.concatenate([t0, t1, t2], axis=1).astype(jnp.bfloat16)
            y = jnp.dot(first_ref[...], x_ref[j], preferred_element_type=jnp.float32).astype(jnp.bfloat16)
            base = pl.multiple_of(16 * b, 16)
            for g in range(16):
                y_ref[g, pl.ds(base, 16)] = y[16 * g:16 * g + 16]
        return carry
    lax.fori_loop(0, 4, residues, 0)

    for g in range(16):
        z = jnp.dot(second_ref[g], y_ref[g], preferred_element_type=jnp.float32)
        for band in range(BANDS):
            for p in range(2):
                r = (band * 2 + p) * 16
                base = 256 * band
                spec_ref[p, base + 8 * g:base + 8 * g + 8] = z[r:r + 8]
                if g == 0:
                    spec_ref[p, base + 249:base + 256] = z[r + 8:r + 15]
                    spec_ref[p, base + 128:base + 129] = z[r + 15:r + 16]
                else:
                    spec_ref[p, base + 249 - 8 * g:base + 257 - 8 * g] = z[r + 8:r + 16]

    mag_ref[0:64] = jnp.zeros((64, LANES), jnp.bfloat16)
    mag_ref[64 + NF:128 + NF] = jnp.zeros((64, LANES), jnp.bfloat16)

    def magnitude(i, carry):
        rows = pl.ds(pl.multiple_of(i * 64, 64), 64)
        re, im = spec_ref[0, rows], spec_ref[1, rows]
        mag_ref[pl.ds(pl.multiple_of(i * 64 + 64, 64), 64)] = jnp.sqrt(re * re + im * im).astype(jnp.bfloat16)
        return carry
    lax.fori_loop(0, NF // 64, magnitude, 0, unroll=4)

    def whiten(band, carry):
        for half in range(2):
            base = pl.multiple_of(band * 256 + 128 * half, 128)
            total = jnp.dot(band_ref[...], mag_ref[pl.ds(base, 256)], preferred_element_type=jnp.float32)
            f = base + lax.broadcasted_iota(jnp.int32, (128, LANES), 0)
            count = (jnp.minimum(f + HW, NF - 1) - jnp.maximum(f - HW, 0) + 1).astype(jnp.float32)
            scale = count / (total + EPSILON * count)
            for p in range(2):
                white = spec_ref[p, pl.ds(base, 128)] * scale
                for t in range(3):
                    turned = jnp.transpose(white[:, 128 * t:128 * t + 128])
                    out_ref[band, p, 128 * t:128 * t + 128, 128 * half:128 * half + 128] = turned.astype(jnp.bfloat16)
        return carry
    lax.fori_loop(0, BANDS, whiten, 0, unroll=4)


def diagonals(arrays, at):
    for bit in (1, 2, 4):
        odd = ((at // 16) & bit) != 0
        arrays = [jnp.where(odd, arrays[(i + bit) % 8], arrays[i]) for i in range(8)]
    return arrays


def cross_kernel(got_ref, out_ref, wide_ref, left_ref, picked_ref, weight_ref, prod_ref):
    step = pl.program_id(0)
    chans = BANDS * OWN

    @pl.when(step == 0)
    def _():
        at = lane((CHANS, 128))

        def gather(src, carry):
            for p in range(2):
                for h in range(2):
                    cols = slice(128 * h, 128 * h + 128)
                    arrays = []
                    for k in range(SEG):
                        x = got_ref[src, p, CHANS * k:CHANS * k + CHANS, cols].astype(jnp.float32)
                        arrays.append(pltpu.roll(x, 16 * k, 1) if k else x)
                    arrays = diagonals(arrays, at)
                    for g in range(8):
                        x = arrays[-g % 8]
                        wide_ref[8 * h + g, pl.ds(pl.multiple_of(OWN * src, 8), OWN), 128 * p:128 * p + 128] = x[:OWN]
                        picked_ref[8 * h + g, pl.ds(pl.multiple_of(PICKED * src, 8), PICKED), 128 * p:128 * p + 128] = x[OWN:] * (1.0 / SEG)
            return carry
        lax.fori_loop(0, BANDS, gather, 0)

        def narrow(g, carry):
            left_ref[g] = wide_ref[g].astype(jnp.bfloat16)
            return carry
        lax.fori_loop(0, 16, narrow, 0, unroll=4)

    same = (lane((16, 256)) % 16) == lax.broadcasted_iota(jnp.int32, (16, 256), 0)
    at = lane((16, 128))

    def multiply(h, g):
        rows = picked_ref[8 * h + g, pl.ds(pl.multiple_of(8 * step, 8), 8)]
        turned = jnp.concatenate([-rows[:, 128:], rows[:, :128]], axis=1)
        for i in range(8):
            q = (i + g) % 8
            for p, values in ((0, rows), (1, turned)):
                wide = jnp.where(same, jnp.broadcast_to(values[i:i + 1], (16, 256)), 0.0)
                weight_ref[h, g, 128 * p + 16 * q:128 * p + 16 * q + 16] = wide.astype(jnp.bfloat16)
        prod = lax.dot_general(left_ref[8 * h + g], weight_ref[h, g], NT, preferred_element_type=jnp.float32)
        prod_ref[h, g] = prod.astype(jnp.bfloat16)

    def place(h, c):
        rows = slice(16 * c, 16 * c + 16)
        for p in range(2):
            arrays = diagonals([prod_ref[h, g, rows, 128 * p:128 * p + 128] for g in range(8)], at)
            for i in range(8):
                x = arrays[-i % 8]
                x = pltpu.roll(x, (-16 * i) % 128, 1) if i else x
                out_ref[p, i, rows, 128 * h:128 * h + 128] = x

    for h in range(2):
        for g in range(8):
            multiply(h, g)
        for c in range(chans // 16):
            place(h, c)


def whole(memory_space=pltpu.VMEM):
    return pl.BlockSpec(memory_space=memory_space)


def shards(records, offsets, sources):
    first, second = step_tables()
    coarse, fine = window_tables()
    blocks = pl.pallas_call(
        pack_kernel,
        out_shape=jax.ShapeDtypeStruct((DEVICES, 56, 128), jnp.bfloat16),
        in_specs=[whole(), whole()],
        out_specs=whole(),
        scratch_shapes=[pltpu.VMEM((8, THIRD, 128), jnp.float32), pltpu.VMEM((8, 8, 128), jnp.float32)],
        compiler_params=pltpu.CompilerParams(vmem_limit_bytes=VMEM),
        name="pack",
    )(sources[None, :], records)
    received = lax.all_to_all(blocks, ("chan", "freq"), split_axis=0, concat_axis=0, tiled=True)
    white = pl.pallas_call(
        spectrum_kernel,
        out_shape=jax.ShapeDtypeStruct((BANDS, 2, LANES, WIDTH), jnp.bfloat16),
        in_specs=[whole(pltpu.SMEM), whole(pltpu.SMEM)] + [whole()] * 5,
        out_specs=whole(),
        scratch_shapes=[
            pltpu.VMEM((ROWS * DEVICES // 16 * 17, 128), jnp.float32),
            pltpu.VMEM((4, 256, LANES), jnp.bfloat16),
            pltpu.VMEM((16, 256, LANES), jnp.bfloat16),
            pltpu.VMEM((2, NF, LANES), jnp.float32),
            pltpu.VMEM((NF + 128, LANES), jnp.bfloat16),
        ],
        compiler_params=pltpu.CompilerParams(vmem_limit_bytes=VMEM),
        name="spectrum",
    )(offsets, fine, received, first, second, band_block(), coarse)
    bands = lax.all_to_all(white, "freq", split_axis=0, concat_axis=0, tiled=True)
    chans = BANDS * OWN
    return pl.pallas_call(
        cross_kernel,
        out_shape=jax.ShapeDtypeStruct((2, NSRC, chans, WIDTH), jnp.bfloat16),
        grid=(NSRC // 8,),
        in_specs=[whole()],
        out_specs=pl.BlockSpec((2, 8, chans, WIDTH), lambda s: (0, s, 0, 0)),
        scratch_shapes=[
            pltpu.VMEM((16, chans, 256), jnp.float32),
            pltpu.VMEM((16, chans, 256), jnp.bfloat16),
            pltpu.VMEM((16, NSRC, 256), jnp.float32),
            pltpu.VMEM((2, 8, 256, 256), jnp.bfloat16),
            pltpu.VMEM((2, 8, chans, 256), jnp.bfloat16),
        ],
        compiler_params=pltpu.CompilerParams(vmem_limit_bytes=VMEM),
        name="cross",
    )(bands)


def solution(mesh):
    in_specs = (P(("chan", "freq"), None), P(), P())
    out_specs = P(None, None, "chan", "freq")
    return jax.shard_map(shards, mesh=mesh, in_specs=in_specs, out_specs=out_specs, check_vma=False)
```

```python
import numpy as np
import jax
import jax.numpy as jnp
import ml_dtypes
from jax import lax
from jax.experimental import pallas as pl
from jax.experimental.pallas import tpu as pltpu
from jax.sharding import PartitionSpec as P

NF = 2048
LENGTH = 2 * NF
SEG = 8
NSRC = 64
HW = 32
EPSILON = 1e-06

DEVICES = 128
ROWS = 144
OWN = 40
PICKED = 8
CHANS = OWN + PICKED
LANES = SEG * CHANS
BANDS = 8
STEP = 16
WIDTH = 256
THIRD = ROWS // 3
VMEM = 56 * 1024 * 1024

NT = (((1,), (1,)), ((), ()))


def step_tables():
    a = np.arange(256)
    first = np.zeros((256, 256))
    for g in range(16):
        for i in range(8):
            f1 = 8 * g + i
            first[16 * g + i] = np.cos(2 * np.pi * ((a * f1) % 256) / 256)
            first[16 * g + 8 + i] = -np.sin(2 * np.pi * ((a * f1) % 256) / 256)
    first[8] = np.cos(np.pi * a)
    b = np.arange(16)
    second = np.zeros((16, 256, 256))
    for g in range(16):
        for band in range(BANDS):
            for j in range(16):
                if j < 8:
                    low = 8 * g + j
                elif g == 0:
                    low = 128 if j == 15 else 249 + j - 8
                else:
                    low = 249 - 8 * g + j - 8
                f = 256 * band + low
                angle = 2 * np.pi * ((b * f) % 4096) / 4096
                c, s = np.cos(angle), np.sin(angle)
                if low <= 128:
                    sign, slot = 1.0, low - 8 * g
                else:
                    sign, slot = -1.0, 256 - low - 8 * g
                row = (band * 2) * 16 + j
                if low == 0:
                    second[g, row, 16 * b] = c
                    second[g, row + 16, 16 * b] = -s
                elif low == 128:
                    second[g, row, 16 * b + 8] = c
                    second[g, row + 16, 16 * b + 8] = -s
                else:
                    second[g, row, 16 * b + slot] = c
                    second[g, row, 16 * b + 8 + slot] = sign * s
                    second[g, row + 16, 16 * b + slot] = -s
                    second[g, row + 16, 16 * b + 8 + slot] = sign * c
    return first.astype(ml_dtypes.bfloat16), second.astype(ml_dtypes.bfloat16)


def window_tables():
    a = np.arange(256) * (2 * np.pi / 256)
    b = np.arange(16) * (2 * np.pi / 4096)
    rows = np.stack([np.cos(a), np.sin(a)])[:, :, None] * np.ones((1, 1, 128))
    return rows.astype(np.float32), np.stack([np.cos(b), np.sin(b)]).astype(np.float32)


def band_block():
    rows = np.arange(128)[:, None] + 64
    return (np.abs(rows - np.arange(256)[None, :]) <= HW).astype(ml_dtypes.bfloat16)


def lane(shape, dtype=jnp.int32):
    return lax.broadcasted_iota(jnp.int32, shape, 1).astype(dtype)


def pack_kernel(sources_ref, records_ref, out_ref, head_ref, tail_ref):
    picked = jnp.zeros((ROWS, NSRC), jnp.float32)
    for i in range(8):
        rows = lax.broadcasted_iota(jnp.int32, (640, NSRC), 0) + 640 * i
        hot = (rows == sources_ref[...]).astype(jnp.bfloat16)
        picked += jnp.dot(records_ref[:, 640 * i:640 * i + 640], hot, preferred_element_type=jnp.float32)
    picked = jnp.concatenate([picked, jnp.zeros((ROWS, 128 - NSRC), jnp.float32)], axis=1)
    at8 = lane((8, 128))
    for band in range(BANDS):
        head_ref[band] = pltpu.roll(picked[:THIRD], (120 - 8 * band) % 128, 1).astype(jnp.bfloat16)
        tail = jnp.zeros((8, 128), jnp.float32)
        for m in range(12):
            piece = pltpu.roll(picked[THIRD + 8 * m:THIRD + 8 * m + 8], (8 * m - 8 * band) % 128, 1)
            tail = jnp.where((at8 >= 8 * m) & (at8 < 8 * m + 8), piece, tail)
        tail_ref[band] = tail
    at = lane((THIRD, 128), jnp.int16)

    def group(i, carry):
        for j in range(16):
            tile, start = divmod(OWN * j, 128)
            parts = []
            for u in range(3):
                shift = (OWN * u - start) % 128

                def piece(t):
                    base = pl.multiple_of(640 * i + 128 * t, 128)
                    x = records_ref[THIRD * u:THIRD * u + THIRD, pl.ds(base, 128)]
                    return pltpu.roll(x, shift, 1) if shift else x
                part = piece(tile)
                if start + OWN > 128:
                    part = jnp.where(at >= OWN * u + 128 - start, piece(tile + 1), part)
                parts.append(part)
            main = jnp.where(at < 40, parts[0], jnp.where(at < 80, parts[1], jnp.where(at < 120, parts[2], head_ref[j % 8])))
            out_ref[16 * i + j, :THIRD] = main
            out_ref[16 * i + j, THIRD:] = tail_ref[j % 8].astype(jnp.bfloat16)
        return carry
    lax.fori_loop(0, 8, group, 0, unroll=2)


def spectrum_kernel(offsets_ref, fine_ref, got_ref, first_ref, second_ref, band_ref, coarse_ref, out_ref,
                    time_ref, x_ref, y_ref, spec_ref, mag_ref):
    own48 = lane((THIRD, 128)) < OWN

    def unpack(src, carry):
        main = got_ref[src, :THIRD]
        tail = got_ref[src].astype(jnp.float32)[THIRD:]
        by48 = pltpu.roll(main, 48, 1).astype(jnp.float32)
        by88 = pltpu.roll(main, 88, 1).astype(jnp.float32)
        main = main.astype(jnp.float32)
        tails = [pltpu.roll(tail, (OWN - 8 * m) % 128, 1) for m in range(12)]
        thirds = [
            jnp.where(own48, main, by48),
            jnp.where(own48, by88, jnp.concatenate(tails[:6], axis=0)),
            jnp.where(own48, by48, jnp.concatenate(tails[6:], axis=0)),
        ]
        for i in range(9):
            time_ref[pl.ds(src * 153 + 17 * i, 16)] = thirds[i // 3][16 * (i % 3):16 * (i % 3) + 16]
        return carry
    lax.fori_loop(0, DEVICES, unpack, 0, unroll=16)

    at = lane((64, 128), jnp.int16)

    def residues(quad, carry):
        for j in range(4):
            b = 4 * quad + j
            cb, sb = fine_ref[0, b], fine_ref[1, b]
            starts = [offsets_ref[k] + b for k in range(SEG)]
            starts = [start + lax.shift_right_logical(start, 4) for start in starts]
            for chunk in range(4):
                rows = slice(64 * chunk, 64 * chunk + 64)
                window = 0.5 - 0.5 * (coarse_ref[0, rows] * cb - coarse_ref[1, rows] * sb)
                placed = []
                for k in range(SEG):
                    piece = (time_ref[pl.ds(starts[k] + 17 * 64 * chunk, 64, 17)] * window).astype(jnp.bfloat16)
                    shift = (CHANS * k) % 128
                    placed.append(pltpu.roll(piece, shift, 1) if shift else piece)
                t0 = jnp.where(at < 48, placed[0], jnp.where(at < 96, placed[1], placed[2]))
                t1 = jnp.where(at < 16, placed[2], jnp.where(at < 64, placed[3], jnp.where(at < 112, placed[4], placed[5])))
                t2 = jnp.where(at < 32, placed[5], jnp.where(at < 80, placed[6], placed[7]))
                x_ref[j, rows] = jnp.concatenate([t0, t1, t2], axis=1)
            y = jnp.dot(first_ref[...], x_ref[j], preferred_element_type=jnp.float32).astype(jnp.bfloat16)
            base = pl.multiple_of(16 * b, 16)
            for g in range(16):
                y_ref[g, pl.ds(base, 16)] = y[16 * g:16 * g + 16]
        return carry
    lax.fori_loop(0, 4, residues, 0)

    for g in range(16):
        z = jnp.dot(second_ref[g], y_ref[g], preferred_element_type=jnp.float32)
        for band in range(BANDS):
            for p in range(2):
                r = (band * 2 + p) * 16
                base = 256 * band
                spec_ref[p, base + 8 * g:base + 8 * g + 8] = z[r:r + 8]
                if g == 0:
                    spec_ref[p, base + 249:base + 256] = z[r + 8:r + 15]
                    spec_ref[p, base + 128:base + 129] = z[r + 15:r + 16]
                else:
                    spec_ref[p, base + 249 - 8 * g:base + 257 - 8 * g] = z[r + 8:r + 16]

    mag_ref[0:64] = jnp.zeros((64, LANES), jnp.bfloat16)
    mag_ref[64 + NF:128 + NF] = jnp.zeros((64, LANES), jnp.bfloat16)

    def magnitude(i, carry):
        rows = pl.ds(pl.multiple_of(i * 64, 64), 64)
        re, im = spec_ref[0, rows], spec_ref[1, rows]
        mag_ref[pl.ds(pl.multiple_of(i * 64 + 64, 64), 64)] = jnp.sqrt(re * re + im * im).astype(jnp.bfloat16)
        return carry
    lax.fori_loop(0, NF // 64, magnitude, 0, unroll=4)

    def whiten(band, carry):
        for half in range(2):
            base = pl.multiple_of(band * 256 + 128 * half, 128)
            total = jnp.dot(band_ref[...], mag_ref[pl.ds(base, 256)], preferred_element_type=jnp.float32)
            f = base + lax.broadcasted_iota(jnp.int32, (128, LANES), 0)
            count = (jnp.minimum(f + HW, NF - 1) - jnp.maximum(f - HW, 0) + 1).astype(jnp.float32)
            scale = count / (total + EPSILON * count)
            for p in range(2):
                white = (spec_ref[p, pl.ds(base, 128)] * scale).astype(jnp.bfloat16)
                for t in range(3):
                    turned = jnp.transpose(white[:, 128 * t:128 * t + 128])
                    out_ref[band, p, 128 * t:128 * t + 128, 128 * half:128 * half + 128] = turned
        return carry
    lax.fori_loop(0, BANDS, whiten, 0, unroll=8)


def diagonals(arrays, at):
    for bit in (1, 2, 4):
        odd = (at & (16 * bit)) != 0
        arrays = [jnp.where(odd, arrays[(i + bit) % 8], arrays[i]) for i in range(8)]
    return arrays


def cross_kernel(got_ref, out_ref, wide_ref, left_ref, picked_ref, prod_ref):
    step = pl.program_id(0)
    chans = BANDS * OWN

    @pl.when(step == 0)
    def _():
        at = lane((CHANS, 128), jnp.int16)

        def gather(src, carry):
            for p in range(2):
                for h in range(2):
                    cols = slice(128 * h, 128 * h + 128)
                    arrays = []
                    for k in range(SEG):
                        x = got_ref[src, p, CHANS * k:CHANS * k + CHANS, cols]
                        arrays.append(pltpu.roll(x, 16 * k, 1) if k else x)
                    arrays = diagonals(arrays, at)
                    for g in range(8):
                        x = arrays[-g % 8].astype(jnp.float32)
                        wide_ref[8 * h + g, pl.ds(pl.multiple_of(OWN * src, 8), OWN), 128 * p:128 * p + 128] = x[:OWN]
                        picked_ref[8 * h + g, pl.ds(pl.multiple_of(PICKED * src, 8), PICKED), 128 * p:128 * p + 128] = x[OWN:] * (1.0 / SEG)
            return carry
        lax.fori_loop(0, BANDS, gather, 0, unroll=4)

        def narrow(g, carry):
            left_ref[g] = wide_ref[g].astype(jnp.bfloat16)
            return carry
        lax.fori_loop(0, 16, narrow, 0, unroll=16)

    same = ((lane((16, 256)) % 16) == lax.broadcasted_iota(jnp.int32, (16, 256), 0)).astype(jnp.bfloat16)
    at = lane((16, 128), jnp.int16)

    def multiply(h, g):
        weight = []
        for part in range(STEP // 8):
            rows = picked_ref[8 * h + g, pl.ds(pl.multiple_of(STEP * step + 8 * part, 8), 8)]
            turned = jnp.concatenate([-rows[:, 128:], rows[:, :128]], axis=1)
            for values in (rows, turned):
                for q in range(8):
                    i = (q - g) % 8
                    weight.append(jnp.broadcast_to(values[i:i + 1], (16, 256)).astype(jnp.bfloat16) * same)
        weight = jnp.concatenate(weight, axis=0)
        prod = lax.dot_general(left_ref[8 * h + g], weight, NT, preferred_element_type=jnp.float32)
        prod_ref[h, g] = prod.astype(jnp.bfloat16)

    def place(h, c):
        rows = slice(16 * c, 16 * c + 16)
        for part in range(STEP // 8):
            for p in range(2):
                lanes = slice(256 * part + 128 * p, 256 * part + 128 * p + 128)
                arrays = diagonals([prod_ref[h, g, rows, lanes] for g in range(8)], at)
                for i in range(8):
                    x = arrays[-i % 8]
                    x = pltpu.roll(x, (-16 * i) % 128, 1) if i else x
                    out_ref[p, 8 * part + i, rows, 128 * h:128 * h + 128] = x

    for h in range(2):
        for g in range(8):
            multiply(h, g)
        for c in range(chans // 16):
            place(h, c)


def whole(memory_space=pltpu.VMEM):
    return pl.BlockSpec(memory_space=memory_space)


def shards(records, offsets, sources):
    first, second = step_tables()
    coarse, fine = window_tables()
    blocks = pl.pallas_call(
        pack_kernel,
        out_shape=jax.ShapeDtypeStruct((DEVICES, 56, 128), jnp.bfloat16),
        in_specs=[whole(), whole()],
        out_specs=whole(),
        scratch_shapes=[pltpu.VMEM((8, THIRD, 128), jnp.bfloat16), pltpu.VMEM((8, 8, 128), jnp.float32)],
        compiler_params=pltpu.CompilerParams(vmem_limit_bytes=VMEM),
        name="pack",
    )(sources[None, :], records)
    received = lax.all_to_all(blocks, ("chan", "freq"), split_axis=0, concat_axis=0, tiled=True)
    white = pl.pallas_call(
        spectrum_kernel,
        out_shape=jax.ShapeDtypeStruct((BANDS, 2, LANES, WIDTH), jnp.bfloat16),
        in_specs=[whole(pltpu.SMEM), whole(pltpu.SMEM)] + [whole()] * 5,
        out_specs=whole(),
        scratch_shapes=[
            pltpu.VMEM((ROWS * DEVICES // 16 * 17, 128), jnp.float32),
            pltpu.VMEM((4, 256, LANES), jnp.bfloat16),
            pltpu.VMEM((16, 256, LANES), jnp.bfloat16),
            pltpu.VMEM((2, NF, LANES), jnp.float32),
            pltpu.VMEM((NF + 128, LANES), jnp.bfloat16),
        ],
        compiler_params=pltpu.CompilerParams(vmem_limit_bytes=VMEM),
        name="spectrum",
    )(offsets, fine, received, first, second, band_block(), coarse)
    bands = lax.all_to_all(white, "freq", split_axis=0, concat_axis=0, tiled=True)
    chans = BANDS * OWN
    return pl.pallas_call(
        cross_kernel,
        out_shape=jax.ShapeDtypeStruct((2, NSRC, chans, WIDTH), jnp.bfloat16),
        grid=(NSRC // STEP,),
        in_specs=[whole()],
        out_specs=pl.BlockSpec((2, STEP, chans, WIDTH), lambda s: (0, s, 0, 0)),
        scratch_shapes=[
            pltpu.VMEM((16, chans, 256), jnp.float32),
            pltpu.VMEM((16, chans, 256), jnp.bfloat16),
            pltpu.VMEM((16, NSRC, 256), jnp.float32),
            pltpu.VMEM((2, 8, chans, 32 * STEP), jnp.bfloat16),
        ],
        compiler_params=pltpu.CompilerParams(vmem_limit_bytes=VMEM),
        name="cross",
    )(bands)


def solution(mesh):
    in_specs = (P(("chan", "freq"), None), P(), P())
    out_specs = P(None, None, "chan", "freq")
    return jax.shard_map(shards, mesh=mesh, in_specs=in_specs, out_specs=out_specs, check_vma=False)
```

```python
import numpy as np
import jax
import jax.numpy as jnp
import ml_dtypes
from jax import lax
from jax.experimental import pallas as pl
from jax.experimental.pallas import tpu as pltpu
from jax.sharding import PartitionSpec as P

NF = 2048
LENGTH = 2 * NF
SEG = 8
NSRC = 64
HW = 32
EPSILON = 1e-06

DEVICES = 128
ROWS = 144
OWN = 40
PICKED = 8
CHANS = OWN + PICKED
LANES = SEG * CHANS
BANDS = 8
STEP = 16
WIDTH = 256
THIRD = ROWS // 3
PARTS = 4
VMEM = 56 * 1024 * 1024

NT = (((1,), (1,)), ((), ()))


def step_tables():
    a = np.arange(256)
    first = np.zeros((256, 256))
    for g in range(16):
        for i in range(8):
            f1 = 8 * g + i
            first[16 * g + i] = np.cos(2 * np.pi * ((a * f1) % 256) / 256)
            first[16 * g + 8 + i] = -np.sin(2 * np.pi * ((a * f1) % 256) / 256)
    first[8] = np.cos(np.pi * a)
    b = np.arange(16)
    second = np.zeros((16, 256, 256))
    for g in range(16):
        for band in range(BANDS):
            for j in range(16):
                if j < 8:
                    low = 8 * g + j
                elif g == 0:
                    low = 128 if j == 15 else 249 + j - 8
                else:
                    low = 249 - 8 * g + j - 8
                f = 256 * band + low
                angle = 2 * np.pi * ((b * f) % 4096) / 4096
                c, s = np.cos(angle), np.sin(angle)
                if low <= 128:
                    sign, slot = 1.0, low - 8 * g
                else:
                    sign, slot = -1.0, 256 - low - 8 * g
                row = (band * 2) * 16 + j
                if low == 0:
                    second[g, row, 16 * b] = c
                    second[g, row + 16, 16 * b] = -s
                elif low == 128:
                    second[g, row, 16 * b + 8] = c
                    second[g, row + 16, 16 * b + 8] = -s
                else:
                    second[g, row, 16 * b + slot] = c
                    second[g, row, 16 * b + 8 + slot] = sign * s
                    second[g, row + 16, 16 * b + slot] = -s
                    second[g, row + 16, 16 * b + 8 + slot] = sign * c
    return first.astype(ml_dtypes.bfloat16), second.astype(ml_dtypes.bfloat16)


def window_tables():
    a = np.arange(256) * (2 * np.pi / 256)
    b = np.arange(16) * (2 * np.pi / 4096)
    rows = np.stack([np.cos(a), np.sin(a)])[:, :, None] * np.ones((1, 1, 128))
    return rows.astype(np.float32), np.stack([np.cos(b), np.sin(b)]).astype(np.float32)


def band_block():
    rows = np.arange(128)[:, None] + 64
    return (np.abs(rows - np.arange(256)[None, :]) <= HW).astype(ml_dtypes.bfloat16)


def lane(shape, dtype=jnp.int32):
    return lax.broadcasted_iota(jnp.int32, shape, 1).astype(dtype)


def pack_kernel(sources_ref, records_ref, out_ref, head_ref, tail_ref):
    picked = jnp.zeros((ROWS, NSRC), jnp.float32)
    for i in range(8):
        rows = lax.broadcasted_iota(jnp.int32, (640, NSRC), 0) + 640 * i
        hot = (rows == sources_ref[...]).astype(jnp.bfloat16)
        picked += jnp.dot(records_ref[:, 640 * i:640 * i + 640], hot, preferred_element_type=jnp.float32)
    picked = jnp.concatenate([picked, jnp.zeros((ROWS, 128 - NSRC), jnp.float32)], axis=1)
    at8 = lane((8, 128))
    for band in range(BANDS):
        head_ref[band] = pltpu.roll(picked[:THIRD], (120 - 8 * band) % 128, 1).astype(jnp.bfloat16)
        tail = jnp.zeros((8, 128), jnp.float32)
        for m in range(12):
            piece = pltpu.roll(picked[THIRD + 8 * m:THIRD + 8 * m + 8], (8 * m - 8 * band) % 128, 1)
            tail = jnp.where((at8 >= 8 * m) & (at8 < 8 * m + 8), piece, tail)
        tail_ref[band] = tail
    at = lane((THIRD, 128), jnp.int16)

    def group(i, carry):
        for j in range(16):
            tile, start = divmod(OWN * j, 128)
            parts = []
            for u in range(3):
                shift = (OWN * u - start) % 128

                def piece(t):
                    base = pl.multiple_of(640 * i + 128 * t, 128)
                    x = records_ref[THIRD * u:THIRD * u + THIRD, pl.ds(base, 128)]
                    return pltpu.roll(x, shift, 1) if shift else x
                part = piece(tile)
                if start + OWN > 128:
                    part = jnp.where(at >= OWN * u + 128 - start, piece(tile + 1), part)
                parts.append(part)
            main = jnp.where(at < 40, parts[0], jnp.where(at < 80, parts[1], jnp.where(at < 120, parts[2], head_ref[j % 8])))
            out_ref[16 * i + j] = jnp.concatenate([main, tail_ref[j % 8].astype(jnp.bfloat16)], axis=0)
        return carry
    lax.fori_loop(0, 8, group, 0, unroll=2)


def spectrum_kernel(offsets_ref, fine_ref, got_hbm, first_ref, second_hbm, band_ref, coarse_ref, out_hbm,
                    got_ref, second_ref, out_ref, got_sem, second_sem, out_sem, time_ref, x_ref, y_ref, spec_ref, mag_ref):
    part = DEVICES // PARTS
    arrivals = [pltpu.make_async_copy(got_hbm.at[pl.ds(part * c, part)], got_ref.at[pl.ds(part * c, part)], got_sem.at[c]) for c in range(PARTS)]
    for copy in arrivals:
        copy.start()
    later = pltpu.make_async_copy(second_hbm, second_ref, second_sem)
    later.start()
    own48 = lane((THIRD, 128)) < OWN

    def unpack(src, carry):
        main = got_ref[src, :THIRD]
        tail = got_ref[src].astype(jnp.float32)[THIRD:]
        by48 = pltpu.roll(main, 48, 1).astype(jnp.float32)
        by88 = pltpu.roll(main, 88, 1).astype(jnp.float32)
        main = main.astype(jnp.float32)
        tails = [pltpu.roll(tail, (OWN - 8 * m) % 128, 1) for m in range(12)]
        thirds = [
            jnp.where(own48, main, by48),
            jnp.where(own48, by88, jnp.concatenate(tails[:6], axis=0)),
            jnp.where(own48, by48, jnp.concatenate(tails[6:], axis=0)),
        ]
        for i in range(9):
            time_ref[pl.ds(src * 153 + 17 * i, 16)] = thirds[i // 3][16 * (i % 3):16 * (i % 3) + 16]
        return carry
    for c in range(PARTS):
        arrivals[c].wait()
        lax.fori_loop(part * c, part * c + part, unpack, 0, unroll=16)

    at = lane((64, 128), jnp.int16)

    def residues(quad, carry):
        for j in range(4):
            b = 4 * quad + j
            cb, sb = fine_ref[0, b], fine_ref[1, b]
            starts = [offsets_ref[k] + b for k in range(SEG)]
            starts = [start + lax.shift_right_logical(start, 4) for start in starts]
            for chunk in range(4):
                rows = slice(64 * chunk, 64 * chunk + 64)
                window = 0.5 - 0.5 * (coarse_ref[0, rows] * cb - coarse_ref[1, rows] * sb)
                placed = []
                for k in range(SEG):
                    piece = (time_ref[pl.ds(starts[k] + 17 * 64 * chunk, 64, 17)] * window).astype(jnp.bfloat16)
                    shift = (CHANS * k) % 128
                    placed.append(pltpu.roll(piece, shift, 1) if shift else piece)
                t0 = jnp.where(at < 48, placed[0], jnp.where(at < 96, placed[1], placed[2]))
                t1 = jnp.where(at < 16, placed[2], jnp.where(at < 64, placed[3], jnp.where(at < 112, placed[4], placed[5])))
                t2 = jnp.where(at < 32, placed[5], jnp.where(at < 80, placed[6], placed[7]))
                x_ref[j // 2, rows, LANES * (j % 2):LANES * (j % 2) + LANES] = jnp.concatenate([t0, t1, t2], axis=1)
            if j % 2:
                y = jnp.dot(first_ref[...], x_ref[j // 2], preferred_element_type=jnp.float32).astype(jnp.bfloat16)
                for i in range(2):
                    base = pl.multiple_of(16 * (b - 1 + i), 16)
                    for g in range(16):
                        y_ref[g, pl.ds(base, 16)] = y[16 * g:16 * g + 16, LANES * i:LANES * i + LANES]
        return carry
    lax.fori_loop(0, 4, residues, 0, unroll=2)

    later.wait()
    for g in range(16):
        z = jnp.dot(second_ref[g], y_ref[g], preferred_element_type=jnp.float32)
        for band in range(BANDS):
            for p in range(2):
                r = (band * 2 + p) * 16
                base = 256 * band
                spec_ref[p, base + 8 * g:base + 8 * g + 8] = z[r:r + 8]
                if g == 0:
                    spec_ref[p, base + 249:base + 256] = z[r + 8:r + 15]
                    spec_ref[p, base + 128:base + 129] = z[r + 15:r + 16]
                else:
                    spec_ref[p, base + 249 - 8 * g:base + 257 - 8 * g] = z[r + 8:r + 16]

    mag_ref[0:64] = jnp.zeros((64, LANES), jnp.bfloat16)
    mag_ref[64 + NF:128 + NF] = jnp.zeros((64, LANES), jnp.bfloat16)

    def magnitude(i, carry):
        rows = pl.ds(pl.multiple_of(i * 64, 64), 64)
        re, im = spec_ref[0, rows], spec_ref[1, rows]
        mag_ref[pl.ds(pl.multiple_of(i * 64 + 64, 64), 64)] = jnp.sqrt(re * re + im * im).astype(jnp.bfloat16)
        return carry
    lax.fori_loop(0, NF // 64, magnitude, 0, unroll=32)

    def whiten(band):
        for half in range(2):
            base = band * 256 + 128 * half
            total = jnp.dot(band_ref[...], mag_ref[pl.ds(base, 256)], preferred_element_type=jnp.float32)
            f = base + lax.broadcasted_iota(jnp.int32, (128, LANES), 0)
            count = (jnp.minimum(f + HW, NF - 1) - jnp.maximum(f - HW, 0) + 1).astype(jnp.float32)
            scale = count / (total + EPSILON * count)
            for p in range(2):
                white = (spec_ref[p, pl.ds(base, 128)] * scale).astype(jnp.bfloat16)
                for t in range(3):
                    turned = jnp.transpose(white[:, 128 * t:128 * t + 128])
                    out_ref[band, p, 128 * t:128 * t + 128, 128 * half:128 * half + 128] = turned

    leaving = []
    for band in range(BANDS):
        whiten(band)
        leaving.append(pltpu.make_async_copy(out_ref.at[band], out_hbm.at[band], out_sem.at[band]))
        leaving[band].start()
    for copy in leaving:
        copy.wait()


def diagonals(arrays, at):
    for bit in (1, 2, 4):
        odd = (at & (16 * bit)) != 0
        arrays = [jnp.where(odd, arrays[(i + bit) % 8], arrays[i]) for i in range(8)]
    return arrays


def cross_kernel(got_hbm, out_ref, got_ref, got_sem, wide_ref, left_ref, picked_ref, prod_ref):
    step = pl.program_id(0)
    chans = BANDS * OWN

    @pl.when(step == 0)
    def _():
        at = lane((CHANS, 128), jnp.int16)
        arrivals = [pltpu.make_async_copy(got_hbm.at[src], got_ref.at[src], got_sem.at[src]) for src in range(BANDS)]
        for copy in arrivals:
            copy.start()

        def gather(src):
            for p in range(2):
                for h in range(2):
                    cols = slice(128 * h, 128 * h + 128)
                    arrays = []
                    for k in range(SEG):
                        x = got_ref[src, p, CHANS * k:CHANS * k + CHANS, cols]
                        arrays.append(pltpu.roll(x, 16 * k, 1) if k else x)
                    arrays = diagonals(arrays, at)
                    for g in range(8):
                        x = arrays[-g % 8].astype(jnp.float32)
                        wide_ref[8 * h + g, pl.ds(OWN * src, OWN), 128 * p:128 * p + 128] = x[:OWN]
                        picked_ref[8 * h + g, pl.ds(PICKED * src, PICKED), 128 * p:128 * p + 128] = x[OWN:] * (1.0 / SEG)
        for src in range(BANDS):
            arrivals[src].wait()
            gather(src)

        def narrow(g, carry):
            left_ref[g] = wide_ref[g].astype(jnp.bfloat16)
            return carry
        lax.fori_loop(0, 16, narrow, 0, unroll=16)

    same = ((lane((16, 256)) % 16) == lax.broadcasted_iota(jnp.int32, (16, 256), 0)).astype(jnp.bfloat16)
    at = lane((16, 128), jnp.int16)

    def multiply(h, g):
        weight = []
        for part in range(STEP // 8):
            rows = picked_ref[8 * h + g, pl.ds(pl.multiple_of(STEP * step + 8 * part, 8), 8)]
            turned = jnp.concatenate([-rows[:, 128:], rows[:, :128]], axis=1)
            for values in (rows, turned):
                for q in range(8):
                    i = (q - g) % 8
                    weight.append(jnp.broadcast_to(values[i:i + 1], (16, 256)).astype(jnp.bfloat16) * same)
        weight = jnp.concatenate(weight, axis=0)
        prod = lax.dot_general(left_ref[8 * h + g], weight, NT, preferred_element_type=jnp.float32)
        prod_ref[h, g] = prod.astype(jnp.bfloat16)

    def place(h, c):
        rows = slice(16 * c, 16 * c + 16)
        for part in range(STEP // 8):
            for p in range(2):
                lanes = slice(256 * part + 128 * p, 256 * part + 128 * p + 128)
                arrays = diagonals([prod_ref[h, g, rows, lanes] for g in range(8)], at)
                for i in range(8):
                    x = arrays[-i % 8]
                    x = pltpu.roll(x, (-16 * i) % 128, 1) if i else x
                    out_ref[p, 8 * part + i, rows, 128 * h:128 * h + 128] = x

    for h in range(2):
        for g in range(8):
            multiply(h, g)
        for c in range(chans // 16):
            place(h, c)


def whole(memory_space=pltpu.VMEM):
    return pl.BlockSpec(memory_space=memory_space)


def shards(records, offsets, sources):
    first, second = step_tables()
    coarse, fine = window_tables()
    blocks = pl.pallas_call(
        pack_kernel,
        out_shape=jax.ShapeDtypeStruct((DEVICES, 56, 128), jnp.bfloat16),
        in_specs=[whole(), whole()],
        out_specs=whole(),
        scratch_shapes=[pltpu.VMEM((8, THIRD, 128), jnp.bfloat16), pltpu.VMEM((8, 8, 128), jnp.float32)],
        compiler_params=pltpu.CompilerParams(vmem_limit_bytes=VMEM),
        name="pack",
    )(sources[None, :], records)
    received = lax.all_to_all(blocks, ("chan", "freq"), split_axis=0, concat_axis=0, tiled=True)
    white = pl.pallas_call(
        spectrum_kernel,
        out_shape=jax.ShapeDtypeStruct((BANDS, 2, LANES, WIDTH), jnp.bfloat16),
        in_specs=[whole(pltpu.SMEM), whole(pltpu.SMEM), whole(pl.ANY), whole(), whole(pl.ANY), whole(), whole()],
        out_specs=whole(pl.ANY),
        scratch_shapes=[
            pltpu.VMEM((DEVICES, 56, 128), jnp.bfloat16),
            pltpu.VMEM((16, 256, 256), jnp.bfloat16),
            pltpu.VMEM((BANDS, 2, LANES, WIDTH), jnp.bfloat16),
            pltpu.SemaphoreType.DMA((PARTS,)),
            pltpu.SemaphoreType.DMA,
            pltpu.SemaphoreType.DMA((BANDS,)),
            pltpu.VMEM((ROWS * DEVICES // 16 * 17, 128), jnp.float32),
            pltpu.VMEM((2, 256, 2 * LANES), jnp.bfloat16),
            pltpu.VMEM((16, 256, LANES), jnp.bfloat16),
            pltpu.VMEM((2, NF, LANES), jnp.float32),
            pltpu.VMEM((NF + 128, LANES), jnp.bfloat16),
        ],
        compiler_params=pltpu.CompilerParams(vmem_limit_bytes=VMEM),
        name="spectrum",
    )(offsets, fine, received, first, second, band_block(), coarse)
    bands = lax.all_to_all(white, "freq", split_axis=0, concat_axis=0, tiled=True)
    chans = BANDS * OWN
    return pl.pallas_call(
        cross_kernel,
        out_shape=jax.ShapeDtypeStruct((2, NSRC, chans, WIDTH), jnp.bfloat16),
        grid=(NSRC // STEP,),
        in_specs=[whole(pl.ANY)],
        out_specs=pl.BlockSpec((2, STEP, chans, WIDTH), lambda s: (0, s, 0, 0)),
        scratch_shapes=[
            pltpu.VMEM((BANDS, 2, LANES, WIDTH), jnp.bfloat16),
            pltpu.SemaphoreType.DMA((BANDS,)),
            pltpu.VMEM((16, chans, 256), jnp.float32),
            pltpu.VMEM((16, chans, 256), jnp.bfloat16),
            pltpu.VMEM((16, NSRC, 256), jnp.float32),
            pltpu.VMEM((2, 8, chans, 32 * STEP), jnp.bfloat16),
        ],
        compiler_params=pltpu.CompilerParams(vmem_limit_bytes=VMEM),
        name="cross",
    )(bands)


def solution(mesh):
    in_specs = (P(("chan", "freq"), None), P(), P())
    out_specs = P(None, None, "chan", "freq")
    return jax.shard_map(shards, mesh=mesh, in_specs=in_specs, out_specs=out_specs, check_vma=False)
```

```python
import numpy as np
import jax
import jax.numpy as jnp
import ml_dtypes
from jax import lax
from jax.experimental import pallas as pl
from jax.experimental.pallas import tpu as pltpu
from jax.sharding import PartitionSpec as P

NF = 2048
LENGTH = 2 * NF
SEG = 8
NSRC = 64
HW = 32
EPSILON = 1e-06

DEVICES = 128
ROWS = 144
OWN = 40
PICKED = 8
CHANS = OWN + PICKED
LANES = SEG * CHANS
BANDS = 8
STEP = 16
WIDTH = 256
THIRD = ROWS // 3
PARTS = 4
VMEM = 56 * 1024 * 1024

NT = (((1,), (1,)), ((), ()))


def step_tables():
    a = np.arange(256)
    first = np.zeros((256, 256))
    for g in range(16):
        for i in range(8):
            f1 = 8 * g + i
            first[16 * g + i] = np.cos(2 * np.pi * ((a * f1) % 256) / 256)
            first[16 * g + 8 + i] = -np.sin(2 * np.pi * ((a * f1) % 256) / 256)
    first[8] = np.cos(np.pi * a)
    b = np.arange(16)
    second = np.zeros((16, 256, 256))
    for g in range(16):
        for band in range(BANDS):
            for j in range(16):
                if j < 8:
                    low = 8 * g + j
                elif g == 0:
                    low = 128 if j == 15 else 249 + j - 8
                else:
                    low = 249 - 8 * g + j - 8
                f = 256 * band + low
                angle = 2 * np.pi * ((b * f) % 4096) / 4096
                c, s = np.cos(angle), np.sin(angle)
                if low <= 128:
                    sign, slot = 1.0, low - 8 * g
                else:
                    sign, slot = -1.0, 256 - low - 8 * g
                row = (band * 2) * 16 + j
                if low == 0:
                    second[g, row, 16 * b] = c
                    second[g, row + 16, 16 * b] = -s
                elif low == 128:
                    second[g, row, 16 * b + 8] = c
                    second[g, row + 16, 16 * b + 8] = -s
                else:
                    second[g, row, 16 * b + slot] = c
                    second[g, row, 16 * b + 8 + slot] = sign * s
                    second[g, row + 16, 16 * b + slot] = -s
                    second[g, row + 16, 16 * b + 8 + slot] = sign * c
    return first.astype(ml_dtypes.bfloat16), second.astype(ml_dtypes.bfloat16)


def window_tables():
    a = np.arange(256) * (2 * np.pi / 256)
    b = np.arange(16) * (2 * np.pi / 4096)
    rows = np.stack([np.cos(a), np.sin(a)])[:, :, None] * np.ones((1, 1, 128))
    return rows.astype(np.float32), np.stack([np.cos(b), np.sin(b)]).astype(np.float32)


def band_block():
    rows = np.arange(128)[:, None] + 64
    return (np.abs(rows - np.arange(256)[None, :]) <= HW).astype(ml_dtypes.bfloat16)


def lane(shape, dtype=jnp.int32):
    return lax.broadcasted_iota(jnp.int32, shape, 1).astype(dtype)


def pack_kernel(sources_ref, records_ref, out_ref, head_ref, tail_ref):
    picked = jnp.zeros((ROWS, NSRC), jnp.float32)
    for i in range(8):
        rows = lax.broadcasted_iota(jnp.int32, (640, NSRC), 0) + 640 * i
        hot = (rows == sources_ref[...]).astype(jnp.bfloat16)
        picked += jnp.dot(records_ref[:, 640 * i:640 * i + 640], hot, preferred_element_type=jnp.float32)
    picked = jnp.concatenate([picked, jnp.zeros((ROWS, 128 - NSRC), jnp.float32)], axis=1)
    at8 = lane((8, 128))
    for band in range(BANDS):
        head_ref[band] = pltpu.roll(picked[:THIRD], (120 - 8 * band) % 128, 1).astype(jnp.bfloat16)
        tail = jnp.zeros((8, 128), jnp.float32)
        for m in range(12):
            piece = pltpu.roll(picked[THIRD + 8 * m:THIRD + 8 * m + 8], (8 * m - 8 * band) % 128, 1)
            tail = jnp.where((at8 >= 8 * m) & (at8 < 8 * m + 8), piece, tail)
        tail_ref[band] = tail
    at = lane((THIRD, 128), jnp.int16)

    def group(i, carry):
        for j in range(16):
            tile, start = divmod(OWN * j, 128)
            parts = []
            for u in range(3):
                shift = (OWN * u - start) % 128

                def piece(t):
                    base = pl.multiple_of(640 * i + 128 * t, 128)
                    x = records_ref[THIRD * u:THIRD * u + THIRD, pl.ds(base, 128)]
                    return pltpu.roll(x, shift, 1) if shift else x
                part = piece(tile)
                if start + OWN > 128:
                    part = jnp.where(at >= OWN * u + 128 - start, piece(tile + 1), part)
                parts.append(part)
            main = jnp.where(at < 40, parts[0], jnp.where(at < 80, parts[1], jnp.where(at < 120, parts[2], head_ref[j % 8])))
            out_ref[16 * i + j] = jnp.concatenate([main, tail_ref[j % 8].astype(jnp.bfloat16)], axis=0)
        return carry
    lax.fori_loop(0, 8, group, 0, unroll=8)


def spectrum_kernel(offsets_ref, fine_ref, got_hbm, first_ref, second_hbm, band_ref, coarse_ref, out_hbm,
                    got_ref, second_ref, out_ref, got_sem, second_sem, out_sem, time_ref, x_ref, y_ref, spec_ref, mag_ref):
    part = DEVICES // PARTS
    arrivals = [pltpu.make_async_copy(got_hbm.at[pl.ds(part * c, part)], got_ref.at[pl.ds(part * c, part)], got_sem.at[c]) for c in range(PARTS)]
    for copy in arrivals:
        copy.start()
    later = pltpu.make_async_copy(second_hbm, second_ref, second_sem)
    later.start()
    own48 = lane((THIRD, 128)) < OWN

    def unpack(src, carry):
        main = got_ref[src, :THIRD]
        tail = got_ref[src].astype(jnp.float32)[THIRD:]
        by48 = pltpu.roll(main, 48, 1).astype(jnp.float32)
        by88 = pltpu.roll(main, 88, 1).astype(jnp.float32)
        main = main.astype(jnp.float32)
        tails = [pltpu.roll(tail, (OWN - 8 * m) % 128, 1) for m in range(12)]
        thirds = [
            jnp.where(own48, main, by48),
            jnp.where(own48, by88, jnp.concatenate(tails[:6], axis=0)),
            jnp.where(own48, by48, jnp.concatenate(tails[6:], axis=0)),
        ]
        for i in range(9):
            time_ref[pl.ds(src * 153 + 17 * i, 16)] = thirds[i // 3][16 * (i % 3):16 * (i % 3) + 16]
        return carry
    for c in range(PARTS):
        arrivals[c].wait()
        lax.fori_loop(part * c, part * c + part, unpack, 0, unroll=32)

    at = lane((64, 128), jnp.int16)

    def residues(quad, carry):
        for j in range(4):
            b = 4 * quad + j
            cb, sb = fine_ref[0, b], fine_ref[1, b]
            starts = [offsets_ref[k] + b for k in range(SEG)]
            starts = [start + lax.shift_right_logical(start, 4) for start in starts]
            for chunk in range(4):
                rows = slice(64 * chunk, 64 * chunk + 64)
                window = 0.5 - 0.5 * (coarse_ref[0, rows] * cb - coarse_ref[1, rows] * sb)
                placed = []
                for k in range(SEG):
                    piece = (time_ref[pl.ds(starts[k] + 17 * 64 * chunk, 64, 17)] * window).astype(jnp.bfloat16)
                    shift = (CHANS * k) % 128
                    placed.append(pltpu.roll(piece, shift, 1) if shift else piece)
                t0 = jnp.where(at < 48, placed[0], jnp.where(at < 96, placed[1], placed[2]))
                t1 = jnp.where(at < 16, placed[2], jnp.where(at < 64, placed[3], jnp.where(at < 112, placed[4], placed[5])))
                t2 = jnp.where(at < 32, placed[5], jnp.where(at < 80, placed[6], placed[7]))
                x_ref[j // 2, rows, LANES * (j % 2):LANES * (j % 2) + LANES] = jnp.concatenate([t0, t1, t2], axis=1)
            if j % 2:
                y = jnp.dot(first_ref[...], x_ref[j // 2], preferred_element_type=jnp.float32).astype(jnp.bfloat16)
                for i in range(2):
                    base = pl.multiple_of(16 * (b - 1 + i), 16)
                    for g in range(16):
                        y_ref[g, pl.ds(base, 16)] = y[16 * g:16 * g + 16, LANES * i:LANES * i + LANES]
        return carry
    lax.fori_loop(0, 4, residues, 0, unroll=4)

    later.wait()
    for g in range(16):
        z = jnp.dot(second_ref[g], y_ref[g], preferred_element_type=jnp.float32)
        for band in range(BANDS):
            for p in range(2):
                r = (band * 2 + p) * 16
                base = 256 * band
                spec_ref[p, base + 8 * g:base + 8 * g + 8] = z[r:r + 8]
                if g == 0:
                    spec_ref[p, base + 249:base + 256] = z[r + 8:r + 15]
                    spec_ref[p, base + 128:base + 129] = z[r + 15:r + 16]
                else:
                    spec_ref[p, base + 249 - 8 * g:base + 257 - 8 * g] = z[r + 8:r + 16]

    mag_ref[0:64] = jnp.zeros((64, LANES), jnp.bfloat16)
    mag_ref[64 + NF:128 + NF] = jnp.zeros((64, LANES), jnp.bfloat16)

    def magnitude(i, carry):
        rows = pl.ds(pl.multiple_of(i * 64, 64), 64)
        re, im = spec_ref[0, rows], spec_ref[1, rows]
        mag_ref[pl.ds(pl.multiple_of(i * 64 + 64, 64), 64)] = jnp.sqrt(re * re + im * im).astype(jnp.bfloat16)
        return carry
    lax.fori_loop(0, NF // 64, magnitude, 0, unroll=32)

    def whiten(band):
        for half in range(2):
            base = band * 256 + 128 * half
            total = jnp.dot(band_ref[...], mag_ref[pl.ds(base, 256)], preferred_element_type=jnp.float32)
            f = base + lax.broadcasted_iota(jnp.int32, (128, LANES), 0)
            count = (jnp.minimum(f + HW, NF - 1) - jnp.maximum(f - HW, 0) + 1).astype(jnp.float32)
            scale = count / (total + EPSILON * count)
            for p in range(2):
                white = (spec_ref[p, pl.ds(base, 128)] * scale).astype(jnp.bfloat16)
                for t in range(3):
                    turned = jnp.transpose(white[:, 128 * t:128 * t + 128])
                    out_ref[band, p, 128 * t:128 * t + 128, 128 * half:128 * half + 128] = turned

    leaving = []
    for band in range(BANDS):
        whiten(band)
        leaving.append(pltpu.make_async_copy(out_ref.at[band], out_hbm.at[band], out_sem.at[band]))
        leaving[band].start()
    for copy in leaving:
        copy.wait()


def diagonals(arrays, at):
    for bit in (1, 2, 4):
        odd = (at & (16 * bit)) != 0
        arrays = [jnp.where(odd, arrays[(i + bit) % 8], arrays[i]) for i in range(8)]
    return arrays


def cross_kernel(got_hbm, out_ref, got_ref, got_sem, wide_ref, left_ref, picked_ref, prod_ref):
    step = pl.program_id(0)
    chans = BANDS * OWN

    @pl.when(step == 0)
    def _():
        at = lane((CHANS, 128), jnp.int16)
        arrivals = [pltpu.make_async_copy(got_hbm.at[src], got_ref.at[src], got_sem.at[src]) for src in range(BANDS)]
        for copy in arrivals:
            copy.start()

        def gather(src):
            for p in range(2):
                for h in range(2):
                    cols = slice(128 * h, 128 * h + 128)
                    arrays = []
                    for k in range(SEG):
                        x = got_ref[src, p, CHANS * k:CHANS * k + CHANS, cols]
                        arrays.append(pltpu.roll(x, 16 * k, 1) if k else x)
                    arrays = diagonals(arrays, at)
                    for g in range(8):
                        x = arrays[-g % 8].astype(jnp.float32)
                        wide_ref[8 * h + g, pl.ds(OWN * src, OWN), 128 * p:128 * p + 128] = x[:OWN]
                        picked_ref[8 * h + g, pl.ds(PICKED * src, PICKED), 128 * p:128 * p + 128] = x[OWN:] * (1.0 / SEG)
        for src in range(BANDS):
            arrivals[src].wait()
            gather(src)

        def narrow(g, carry):
            left_ref[g] = wide_ref[g].astype(jnp.bfloat16)
            return carry
        lax.fori_loop(0, 16, narrow, 0, unroll=16)

    same = ((lane((16, 256)) % 16) == lax.broadcasted_iota(jnp.int32, (16, 256), 0)).astype(jnp.bfloat16)
    at = lane((16, 128), jnp.int16)

    def multiply(slot, h, g):
        weight = []
        for part in range(STEP // 8):
            rows = picked_ref[8 * h + g, pl.ds(pl.multiple_of(STEP * step + 8 * part, 8), 8)]
            turned = jnp.concatenate([-rows[:, 128:], rows[:, :128]], axis=1)
            for values in (rows, turned):
                for q in range(8):
                    i = (q - g) % 8
                    weight.append(jnp.broadcast_to(values[i:i + 1], (16, 256)).astype(jnp.bfloat16) * same)
        weight = jnp.concatenate(weight, axis=0)
        prod = lax.dot_general(left_ref[8 * h + g], weight, NT, preferred_element_type=jnp.float32)
        prod_ref[slot, h, g] = prod.astype(jnp.bfloat16)

    def place(slot, h, c):
        rows = slice(16 * c, 16 * c + 16)
        for part in range(STEP // 8):
            for p in range(2):
                lanes = slice(256 * part + 128 * p, 256 * part + 128 * p + 128)
                arrays = diagonals([prod_ref[slot, h, g, rows, lanes] for g in range(8)], at)
                for i in range(8):
                    x = arrays[-i % 8]
                    x = pltpu.roll(x, (-16 * i) % 128, 1) if i else x
                    out_ref[p, 8 * part + i, rows, 128 * h:128 * h + 128] = x

    def work(multiplied, placed):
        for h in range(2):
            if multiplied is not None:
                for g in range(8):
                    multiply(multiplied, h, g)
            if placed is not None:
                for c in range(chans // 16):
                    place(placed, h, c)

    last = NSRC // STEP

    @pl.when(step == 0)
    def _():
        work(0, None)

    @pl.when((step > 0) & (step < last) & (step % 2 == 0))
    def _():
        work(0, 1)

    @pl.when((step < last) & (step % 2 == 1))
    def _():
        work(1, 0)

    @pl.when(step == last)
    def _():
        work(None, (last - 1) % 2)


def whole(memory_space=pltpu.VMEM):
    return pl.BlockSpec(memory_space=memory_space)


def shards(records, offsets, sources):
    first, second = step_tables()
    coarse, fine = window_tables()
    blocks = pl.pallas_call(
        pack_kernel,
        out_shape=jax.ShapeDtypeStruct((DEVICES, 56, 128), jnp.bfloat16),
        in_specs=[whole(), whole()],
        out_specs=whole(),
        scratch_shapes=[pltpu.VMEM((8, THIRD, 128), jnp.bfloat16), pltpu.VMEM((8, 8, 128), jnp.float32)],
        compiler_params=pltpu.CompilerParams(vmem_limit_bytes=VMEM),
        name="pack",
    )(sources[None, :], records)
    received = lax.all_to_all(blocks, ("chan", "freq"), split_axis=0, concat_axis=0, tiled=True)
    white = pl.pallas_call(
        spectrum_kernel,
        out_shape=jax.ShapeDtypeStruct((BANDS, 2, LANES, WIDTH), jnp.bfloat16),
        in_specs=[whole(pltpu.SMEM), whole(pltpu.SMEM), whole(pl.ANY), whole(), whole(pl.ANY), whole(), whole()],
        out_specs=whole(pl.ANY),
        scratch_shapes=[
            pltpu.VMEM((DEVICES, 56, 128), jnp.bfloat16),
            pltpu.VMEM((16, 256, 256), jnp.bfloat16),
            pltpu.VMEM((BANDS, 2, LANES, WIDTH), jnp.bfloat16),
            pltpu.SemaphoreType.DMA((PARTS,)),
            pltpu.SemaphoreType.DMA,
            pltpu.SemaphoreType.DMA((BANDS,)),
            pltpu.VMEM((ROWS * DEVICES // 16 * 17, 128), jnp.float32),
            pltpu.VMEM((2, 256, 2 * LANES), jnp.bfloat16),
            pltpu.VMEM((16, 256, LANES), jnp.bfloat16),
            pltpu.VMEM((2, NF, LANES), jnp.float32),
            pltpu.VMEM((NF + 128, LANES), jnp.bfloat16),
        ],
        compiler_params=pltpu.CompilerParams(vmem_limit_bytes=VMEM),
        name="spectrum",
    )(offsets, fine, received, first, second, band_block(), coarse)
    bands = lax.all_to_all(white, "freq", split_axis=0, concat_axis=0, tiled=True)
    chans = BANDS * OWN
    return pl.pallas_call(
        cross_kernel,
        out_shape=jax.ShapeDtypeStruct((2, NSRC, chans, WIDTH), jnp.bfloat16),
        grid=(NSRC // STEP + 1,),
        in_specs=[whole(pl.ANY)],
        out_specs=pl.BlockSpec((2, STEP, chans, WIDTH), lambda s: (0, jnp.maximum(s - 1, 0), 0, 0)),
        scratch_shapes=[
            pltpu.VMEM((BANDS, 2, LANES, WIDTH), jnp.bfloat16),
            pltpu.SemaphoreType.DMA((BANDS,)),
            pltpu.VMEM((16, chans, 256), jnp.float32),
            pltpu.VMEM((16, chans, 256), jnp.bfloat16),
            pltpu.VMEM((16, NSRC, 256), jnp.float32),
            pltpu.VMEM((2, 2, 8, chans, 32 * STEP), jnp.bfloat16),
        ],
        compiler_params=pltpu.CompilerParams(vmem_limit_bytes=VMEM),
        name="cross",
    )(bands)


def solution(mesh):
    in_specs = (P(("chan", "freq"), None), P(), P())
    out_specs = P(None, None, "chan", "freq")
    return jax.shard_map(shards, mesh=mesh, in_specs=in_specs, out_specs=out_specs, check_vma=False)
```

```python
import numpy as np
import jax
import jax.numpy as jnp
import ml_dtypes
from jax import lax
from jax.experimental import pallas as pl
from jax.experimental.pallas import tpu as pltpu
from jax.sharding import PartitionSpec as P

NF = 2048
LENGTH = 2 * NF
SEG = 8
NSRC = 64
HW = 32
EPSILON = 1e-06

DEVICES = 128
ROWS = 144
OWN = 40
PICKED = 8
CHANS = OWN + PICKED
LANES = SEG * CHANS
BANDS = 8
STEP = 16
WIDTH = 256
THIRD = ROWS // 3
PARTS = 4
VMEM = 56 * 1024 * 1024

NT = (((1,), (1,)), ((), ()))


def step_tables():
    a = np.arange(256)
    first = np.zeros((256, 256))
    for g in range(16):
        for i in range(8):
            f1 = 8 * g + i
            first[16 * g + i] = np.cos(2 * np.pi * ((a * f1) % 256) / 256)
            first[16 * g + 8 + i] = -np.sin(2 * np.pi * ((a * f1) % 256) / 256)
    first[8] = np.cos(np.pi * a)
    b = np.arange(16)
    second = np.zeros((16, 256, 256))
    for g in range(16):
        for band in range(BANDS):
            for j in range(16):
                if j < 8:
                    low = 8 * g + j
                elif g == 0:
                    low = 128 if j == 15 else 249 + j - 8
                else:
                    low = 249 - 8 * g + j - 8
                f = 256 * band + low
                angle = 2 * np.pi * ((b * f) % 4096) / 4096
                c, s = np.cos(angle), np.sin(angle)
                if low <= 128:
                    sign, slot = 1.0, low - 8 * g
                else:
                    sign, slot = -1.0, 256 - low - 8 * g
                row = (band * 2) * 16 + j
                if low == 0:
                    second[g, row, 16 * b] = c
                    second[g, row + 16, 16 * b] = -s
                elif low == 128:
                    second[g, row, 16 * b + 8] = c
                    second[g, row + 16, 16 * b + 8] = -s
                else:
                    second[g, row, 16 * b + slot] = c
                    second[g, row, 16 * b + 8 + slot] = sign * s
                    second[g, row + 16, 16 * b + slot] = -s
                    second[g, row + 16, 16 * b + 8 + slot] = sign * c
    return first.astype(ml_dtypes.bfloat16), second.astype(ml_dtypes.bfloat16)


def window_tables():
    a = np.arange(256) * (2 * np.pi / 256)
    b = np.arange(16) * (2 * np.pi / 4096)
    rows = np.stack([np.cos(a), np.sin(a)])[:, :, None] * np.ones((1, 1, 128))
    return rows.astype(np.float32), np.stack([np.cos(b), np.sin(b)]).astype(np.float32)


def band_block():
    rows = np.arange(128)[:, None] + 64
    return (np.abs(rows - np.arange(256)[None, :]) <= HW).astype(ml_dtypes.bfloat16)


def lane(shape, dtype=jnp.int32):
    return lax.broadcasted_iota(jnp.int32, shape, 1).astype(dtype)


def pack_kernel(sources_ref, records_ref, out_ref, head_ref, tail_ref):
    picked = jnp.zeros((ROWS, NSRC), jnp.float32)
    for i in range(8):
        rows = lax.broadcasted_iota(jnp.int32, (640, NSRC), 0) + 640 * i
        hot = (rows == sources_ref[...]).astype(jnp.bfloat16)
        picked += jnp.dot(records_ref[:, 640 * i:640 * i + 640], hot, preferred_element_type=jnp.float32)
    picked = jnp.concatenate([picked, jnp.zeros((ROWS, 128 - NSRC), jnp.float32)], axis=1)
    at8 = lane((8, 128))
    for band in range(BANDS):
        head_ref[band] = pltpu.roll(picked[:THIRD], (120 - 8 * band) % 128, 1).astype(jnp.bfloat16)
        tail = jnp.zeros((8, 128), jnp.float32)
        for m in range(12):
            piece = pltpu.roll(picked[THIRD + 8 * m:THIRD + 8 * m + 8], (8 * m - 8 * band) % 128, 1)
            tail = jnp.where((at8 >= 8 * m) & (at8 < 8 * m + 8), piece, tail)
        tail_ref[band] = tail
    at = lane((THIRD, 128), jnp.int16)

    def group(i, carry):
        for j in range(16):
            tile, start = divmod(OWN * j, 128)
            parts = []
            for u in range(3):
                shift = (OWN * u - start) % 128

                def piece(t):
                    base = pl.multiple_of(640 * i + 128 * t, 128)
                    x = records_ref[THIRD * u:THIRD * u + THIRD, pl.ds(base, 128)]
                    return pltpu.roll(x, shift, 1) if shift else x
                part = piece(tile)
                if start + OWN > 128:
                    part = jnp.where(at >= OWN * u + 128 - start, piece(tile + 1), part)
                parts.append(part)
            main = jnp.where(at < 40, parts[0], jnp.where(at < 80, parts[1], jnp.where(at < 120, parts[2], head_ref[j % 8])))
            out_ref[16 * i + j] = jnp.concatenate([main, tail_ref[j % 8].astype(jnp.bfloat16)], axis=0)
        return carry
    lax.fori_loop(0, 8, group, 0, unroll=8)


def spectrum_kernel(offsets_ref, fine_ref, got_hbm, first_ref, second_hbm, band_ref, coarse_ref, out_hbm,
                    got_ref, second_ref, out_ref, got_sem, second_sem, out_sem, time_ref, x_ref, y_ref, spec_ref, mag_ref):
    part = DEVICES // PARTS
    arrivals = [pltpu.make_async_copy(got_hbm.at[pl.ds(part * c, part)], got_ref.at[pl.ds(part * c, part)], got_sem.at[c]) for c in range(PARTS)]
    for copy in arrivals:
        copy.start()
    later = pltpu.make_async_copy(second_hbm, second_ref, second_sem)
    later.start()
    own48 = lane((THIRD, 128)) < OWN

    def unpack(src, carry):
        main = got_ref[src, :THIRD]
        tail = got_ref[src].astype(jnp.float32)[THIRD:]
        by48 = pltpu.roll(main, 48, 1).astype(jnp.float32)
        by88 = pltpu.roll(main, 88, 1).astype(jnp.float32)
        main = main.astype(jnp.float32)
        tails = [pltpu.roll(tail, (OWN - 8 * m) % 128, 1) for m in range(12)]
        thirds = [
            jnp.where(own48, main, by48),
            jnp.where(own48, by88, jnp.concatenate(tails[:6], axis=0)),
            jnp.where(own48, by48, jnp.concatenate(tails[6:], axis=0)),
        ]
        for i in range(9):
            time_ref[pl.ds(src * 153 + 17 * i, 16)] = thirds[i // 3][16 * (i % 3):16 * (i % 3) + 16]
        return carry
    for c in range(PARTS):
        arrivals[c].wait()
        lax.fori_loop(part * c, part * c + part, unpack, 0, unroll=32)

    at = lane((64, 128), jnp.int16)

    def residues(quad, carry):
        for j in range(4):
            b = 4 * quad + j
            cb, sb = fine_ref[0, b], fine_ref[1, b]
            starts = [offsets_ref[k] + b for k in range(SEG)]
            starts = [start + lax.shift_right_logical(start, 4) for start in starts]
            for chunk in range(4):
                rows = slice(64 * chunk, 64 * chunk + 64)
                window = 0.5 - 0.5 * (coarse_ref[0, rows] * cb - coarse_ref[1, rows] * sb)
                placed = []
                for k in range(SEG):
                    piece = (time_ref[pl.ds(starts[k] + 17 * 64 * chunk, 64, 17)] * window).astype(jnp.bfloat16)
                    shift = (CHANS * k) % 128
                    placed.append(pltpu.roll(piece, shift, 1) if shift else piece)
                t0 = jnp.where(at < 48, placed[0], jnp.where(at < 96, placed[1], placed[2]))
                t1 = jnp.where(at < 16, placed[2], jnp.where(at < 64, placed[3], jnp.where(at < 112, placed[4], placed[5])))
                t2 = jnp.where(at < 32, placed[5], jnp.where(at < 80, placed[6], placed[7]))
                x_ref[j // 2, rows, LANES * (j % 2):LANES * (j % 2) + LANES] = jnp.concatenate([t0, t1, t2], axis=1)
            if j % 2:
                y = jnp.dot(first_ref[...], x_ref[j // 2], preferred_element_type=jnp.float32).astype(jnp.bfloat16)
                for i in range(2):
                    base = pl.multiple_of(16 * (b - 1 + i), 16)
                    for g in range(16):
                        y_ref[g, pl.ds(base, 16)] = y[16 * g:16 * g + 16, LANES * i:LANES * i + LANES]
        return carry
    lax.fori_loop(0, 4, residues, 0, unroll=4)

    later.wait()
    for g in range(16):
        z = jnp.dot(second_ref[g], y_ref[g], preferred_element_type=jnp.float32)
        for band in range(BANDS):
            for p in range(2):
                r = (band * 2 + p) * 16
                base = 256 * band
                spec_ref[p, base + 8 * g:base + 8 * g + 8] = z[r:r + 8]
                if g == 0:
                    spec_ref[p, base + 249:base + 256] = z[r + 8:r + 15]
                    spec_ref[p, base + 128:base + 129] = z[r + 15:r + 16]
                else:
                    spec_ref[p, base + 249 - 8 * g:base + 257 - 8 * g] = z[r + 8:r + 16]

    mag_ref[0:64] = jnp.zeros((64, LANES), jnp.bfloat16)
    mag_ref[64 + NF:128 + NF] = jnp.zeros((64, LANES), jnp.bfloat16)

    def magnitude(i, carry):
        rows = pl.ds(pl.multiple_of(i * 64, 64), 64)
        re, im = spec_ref[0, rows], spec_ref[1, rows]
        mag_ref[pl.ds(pl.multiple_of(i * 64 + 64, 64), 64)] = jnp.sqrt(re * re + im * im).astype(jnp.bfloat16)
        return carry
    lax.fori_loop(0, NF // 64, magnitude, 0, unroll=32)

    def whiten(band):
        for half in range(2):
            base = band * 256 + 128 * half
            total = jnp.dot(band_ref[...], mag_ref[pl.ds(base, 256)], preferred_element_type=jnp.float32)
            f = base + lax.broadcasted_iota(jnp.int32, (128, LANES), 0)
            count = (jnp.minimum(f + HW, NF - 1) - jnp.maximum(f - HW, 0) + 1).astype(jnp.float32)
            scale = count / (total + EPSILON * count)
            for p in range(2):
                white = (spec_ref[p, pl.ds(base, 128)] * scale).astype(jnp.bfloat16)
                for t in range(3):
                    turned = jnp.transpose(white[:, 128 * t:128 * t + 128])
                    out_ref[band, p, 128 * t:128 * t + 128, 128 * half:128 * half + 128] = turned

    leaving = []
    for band in range(BANDS):
        whiten(band)
        leaving.append(pltpu.make_async_copy(out_ref.at[band], out_hbm.at[band], out_sem.at[band]))
        leaving[band].start()
    for copy in leaving:
        copy.wait()


def diagonals(arrays, at):
    for bit in (1, 2, 4):
        odd = (at & (16 * bit)) != 0
        arrays = [jnp.where(odd, arrays[(i + bit) % 8], arrays[i]) for i in range(8)]
    return arrays


def cross_kernel(got_hbm, out_ref, got_ref, got_sem, left_ref, picked_ref, prod_ref):
    step = pl.program_id(0)
    chans = BANDS * OWN

    @pl.when(step == 0)
    def _():
        at = lane((CHANS, 128), jnp.int16)
        arrivals = [pltpu.make_async_copy(got_hbm.at[src], got_ref.at[src], got_sem.at[src]) for src in range(BANDS)]
        for copy in arrivals:
            copy.start()

        def gather(pair):
            for p in range(2):
                for h in range(2):
                    cols, half = slice(128 * h, 128 * h + 128), slice(128 * p, 128 * p + 128)
                    both = []
                    for src in (2 * pair, 2 * pair + 1):
                        arrays = []
                        for k in range(SEG):
                            x = got_ref[src, p, CHANS * k:CHANS * k + CHANS, cols]
                            arrays.append(pltpu.roll(x, 16 * k, 1) if k else x)
                        arrays = diagonals(arrays, at)
                        both.append([arrays[-g % 8].astype(jnp.float32) for g in range(8)])
                        for g in range(8):
                            picked_ref[8 * h + g, PICKED * src:PICKED * src + PICKED, half] = both[-1][g][OWN:] * (1.0 / SEG)
                    for g in range(8):
                        x = jnp.concatenate([both[0][g][:OWN], both[1][g][:OWN]], axis=0)
                        left_ref[8 * h + g, 2 * OWN * pair:2 * OWN * pair + 2 * OWN, half] = x.astype(jnp.bfloat16)
        for pair in range(BANDS // 2):
            arrivals[2 * pair].wait()
            arrivals[2 * pair + 1].wait()
            gather(pair)

    same = ((lane((16, 256)) % 16) == lax.broadcasted_iota(jnp.int32, (16, 256), 0)).astype(jnp.bfloat16)
    at = lane((16, 128), jnp.int16)

    def multiply(slot, h, g):
        weight = []
        for part in range(STEP // 8):
            rows = picked_ref[8 * h + g, pl.ds(pl.multiple_of(STEP * step + 8 * part, 8), 8)]
            turned = jnp.concatenate([-rows[:, 128:], rows[:, :128]], axis=1)
            for values in (rows, turned):
                for q in range(8):
                    i = (q - g) % 8
                    weight.append(jnp.broadcast_to(values[i:i + 1], (16, 256)).astype(jnp.bfloat16) * same)
        weight = jnp.concatenate(weight, axis=0)
        prod = lax.dot_general(left_ref[8 * h + g], weight, NT, preferred_element_type=jnp.float32)
        prod_ref[slot, h, g] = prod.astype(jnp.bfloat16)

    def place(slot, h, c):
        rows = slice(16 * c, 16 * c + 16)
        for part in range(STEP // 8):
            for p in range(2):
                lanes = slice(256 * part + 128 * p, 256 * part + 128 * p + 128)
                arrays = diagonals([prod_ref[slot, h, g, rows, lanes] for g in range(8)], at)
                for i in range(8):
                    x = arrays[-i % 8]
                    x = pltpu.roll(x, (-16 * i) % 128, 1) if i else x
                    out_ref[p, 8 * part + i, rows, 128 * h:128 * h + 128] = x

    def work(multiplied, placed):
        for h in range(2):
            if multiplied is not None:
                for g in range(8):
                    multiply(multiplied, h, g)
            if placed is not None:
                for c in range(chans // 16):
                    place(placed, h, c)

    last = NSRC // STEP

    @pl.when(step == 0)
    def _():
        work(0, None)

    @pl.when((step > 0) & (step < last) & (step % 2 == 0))
    def _():
        work(0, 1)

    @pl.when((step < last) & (step % 2 == 1))
    def _():
        work(1, 0)

    @pl.when(step == last)
    def _():
        work(None, (last - 1) % 2)


def whole(memory_space=pltpu.VMEM):
    return pl.BlockSpec(memory_space=memory_space)


def shards(records, offsets, sources):
    first, second = step_tables()
    coarse, fine = window_tables()
    blocks = pl.pallas_call(
        pack_kernel,
        out_shape=jax.ShapeDtypeStruct((DEVICES, 56, 128), jnp.bfloat16),
        in_specs=[whole(), whole()],
        out_specs=whole(),
        scratch_shapes=[pltpu.VMEM((8, THIRD, 128), jnp.bfloat16), pltpu.VMEM((8, 8, 128), jnp.float32)],
        compiler_params=pltpu.CompilerParams(vmem_limit_bytes=VMEM),
        name="pack",
    )(sources[None, :], records)
    received = lax.all_to_all(blocks, ("chan", "freq"), split_axis=0, concat_axis=0, tiled=True)
    white = pl.pallas_call(
        spectrum_kernel,
        out_shape=jax.ShapeDtypeStruct((BANDS, 2, LANES, WIDTH), jnp.bfloat16),
        in_specs=[whole(pltpu.SMEM), whole(pltpu.SMEM), whole(pl.ANY), whole(), whole(pl.ANY), whole(), whole()],
        out_specs=whole(pl.ANY),
        scratch_shapes=[
            pltpu.VMEM((DEVICES, 56, 128), jnp.bfloat16),
            pltpu.VMEM((16, 256, 256), jnp.bfloat16),
            pltpu.VMEM((BANDS, 2, LANES, WIDTH), jnp.bfloat16),
            pltpu.SemaphoreType.DMA((PARTS,)),
            pltpu.SemaphoreType.DMA,
            pltpu.SemaphoreType.DMA((BANDS,)),
            pltpu.VMEM((ROWS * DEVICES // 16 * 17, 128), jnp.float32),
            pltpu.VMEM((2, 256, 2 * LANES), jnp.bfloat16),
            pltpu.VMEM((16, 256, LANES), jnp.bfloat16),
            pltpu.VMEM((2, NF, LANES), jnp.float32),
            pltpu.VMEM((NF + 128, LANES), jnp.bfloat16),
        ],
        compiler_params=pltpu.CompilerParams(vmem_limit_bytes=VMEM),
        name="spectrum",
    )(offsets, fine, received, first, second, band_block(), coarse)
    bands = lax.all_to_all(white, "freq", split_axis=0, concat_axis=0, tiled=True)
    chans = BANDS * OWN
    return pl.pallas_call(
        cross_kernel,
        out_shape=jax.ShapeDtypeStruct((2, NSRC, chans, WIDTH), jnp.bfloat16),
        grid=(NSRC // STEP + 1,),
        in_specs=[whole(pl.ANY)],
        out_specs=pl.BlockSpec((2, STEP, chans, WIDTH), lambda s: (0, jnp.maximum(s - 1, 0), 0, 0)),
        scratch_shapes=[
            pltpu.VMEM((BANDS, 2, LANES, WIDTH), jnp.bfloat16),
            pltpu.SemaphoreType.DMA((BANDS,)),
            pltpu.VMEM((16, chans, 256), jnp.bfloat16),
            pltpu.VMEM((16, NSRC, 256), jnp.float32),
            pltpu.VMEM((2, 2, 8, chans, 32 * STEP), jnp.bfloat16),
        ],
        compiler_params=pltpu.CompilerParams(vmem_limit_bytes=VMEM),
        name="cross",
    )(bands)


def solution(mesh):
    in_specs = (P(("chan", "freq"), None), P(), P())
    out_specs = P(None, None, "chan", "freq")
    return jax.shard_map(shards, mesh=mesh, in_specs=in_specs, out_specs=out_specs, check_vma=False)
```
